256 devices in a mesh: hx: 16 (over z, y_hi), hy: 8 (over x, core), ga: 2 (over y_lo).
Axes of the slice: x: 4, y: 4 (y_hi: 2, y_lo: 2; y = y_hi * 2 + y_lo), z: 8, core: 2. Of those that a mesh axis runs over, the one named last changes fastest.
Arguments:
- density: float32 [128, 256, 256], P('hx', 'hy', 'ga'), may hold values from 0.5 to 2
- velocity: float32 [3, 128, 256, 256], P(None, 'hx', 'hy', 'ga'), may hold values from -3 to 3
- pressure: float32 [128, 256, 256], P('hx', 'hy', 'ga'), may hold values from 0.3 to 3
- species: float32 [9, 128, 256, 256], P(None, 'hx', 'hy', 'ga'), may hold values from 0.05 to 1
- newton_count: int32 [128, 256, 256], P('hx', 'hy', 'ga'), may hold values from 1 to 4
Outputs:
- new_density: float32 [128, 256, 256], P('hx', 'hy', 'ga')
- momentum: float32 [3, 128, 256, 256], P(None, 'hx', 'hy', 'ga')
- total_energy: float32 [128, 256, 256], P('hx', 'hy', 'ga')
- species_mass: float32 [9, 128, 256, 256], P(None, 'hx', 'hy', 'ga')
- potential: float32 [128, 256, 256], P('hx', 'hy', 'ga')
The draws below stay inside these ranges and needn't reach their ends.
Inputs may be any that keep to these rules, and one draw needn't show every extreme that they name: `newton_count`: how many Newton iterations each cell takes.
All inputs are finite; a program needn't handle non-finite values.
Results may differ from the reference program's by a relative error of at most 0.0003.
Values sent between devices are 32-bit elements; how exact they have to be, the bound alone decides.
A program may use at most 128 MiB of HBM per device.

```python
import math
import jax
import jax.numpy as jnp
from jax import lax

BX = 8
NEWTON = 4
NX = 128
NY = 256
NZ = 256
N_HX = 16


def place_ends(entries, rng, smallest, largest):
    shape = entries.shape
    spot = [jax.random.randint(jax.random.fold_in(rng, axis), (), 0, shape[axis]) for axis in range(len(shape))]
    entries = entries.at[tuple(spot)].set(smallest)
    longest = shape.index(max(shape))
    spot[longest] = (spot[longest] + 1) % shape[longest]
    return entries.at[tuple(spot)].set(largest)


def steps_of(rng, shape, pieces, least, largest):
    loudness, own = 1.0, jax.random.fold_in(rng, 6)
    for position, blocks in pieces:
        steps = jnp.exp(jax.random.uniform(jax.random.fold_in(own, position), (blocks,), jnp.float32, least / len(pieces), largest / len(pieces)))
        loudness = loudness * jnp.repeat(steps, shape[position] // blocks).reshape([-1 if axis == position else 1 for axis in range(len(shape))])
    return loudness


def gaussian(key, shape, scale, reach, shards=(), kind=jnp.bfloat16):
    gain = steps_of(key, shape, shards, -0.22, 0.18) if shards else 1.0
    entries = jax.random.normal(key, shape, jnp.float32) * scale * gain
    return jnp.minimum(jnp.maximum(entries, -reach), reach).astype(kind)


def setup_inputs(seed: int = 0) -> dict:
    seeds = jax.random.split(jax.random.key(seed), 6)
    density = jnp.clip(jnp.exp(math.log(2.0) - 1.3862944 * jax.random.uniform(seeds[0], (NX, NY, NZ), jnp.float32) ** steps_of(seeds[0], (NX, NY, NZ), ((0, 16), (1, 8), (2, 2)), -0.2, 0.2)), 0.5, 2.0)
    velocity = gaussian(seeds[1], (3, NX, NY, NZ), 0.5, 3.0, ((1, 16), (2, 8), (3, 2)), jnp.float32)
    pressure = jnp.clip(jnp.exp(math.log(3.0) - 2.3025851 * jax.random.uniform(seeds[2], (NX, NY, NZ), jnp.float32) ** steps_of(seeds[2], (NX, NY, NZ), ((0, 16), (1, 8), (2, 2)), -0.2, 0.2)), 0.3, 3.0)
    species = jnp.clip(0.05 + 0.95 * jax.random.uniform(seeds[3], (9, NX, NY, NZ), jnp.float32) ** steps_of(seeds[3], (9, NX, NY, NZ), ((1, 16), (2, 8), (3, 2)), -0.2, 0.2), 0.05, 1.0)
    newton_count = place_ends(jax.random.randint(seeds[4], (NX, NY, NZ), 1, 5), jax.random.fold_in(seeds[4], 1), 1, 4).astype(jnp.int32)
    return {"density": density, "velocity": velocity, "pressure": pressure, "species": species, "newton_count": newton_count}


gamma_gas = 5.0 / 3.0
time_step = 0.1
cool_rates = (2.0, 5.0, 9.0, 14.0, 20.0, 3.0, 7.0, 11.0, 29.0)

def cooled_pressure(density, pressure, species, newton_count):
    cooling = cool_rates[0] * species[0]
    for species_index in range(1, 9):
        cooling = cooling + cool_rates[species_index] * species[species_index]
    stiffness = time_step * density * cooling
    initial = pressure / ((gamma_gas - 1.0) * density)
    energy = initial
    for newton_step in range(NEWTON):
        residual_value = energy - initial + stiffness * energy * energy / (1.0 + energy)
        derivative = 1.0 + stiffness * energy * (energy + 2.0) / ((1.0 + energy) * (1.0 + energy))
        energy = jnp.where(newton_count > newton_step, energy - residual_value / derivative, energy)
    return (gamma_gas - 1.0) * density * energy

def conserved(primitive):
    density = primitive[0]
    velocity = primitive[1:4]
    kinetic = 0.5 * density * (velocity[0] * velocity[0] + velocity[1] * velocity[1] + velocity[2] * velocity[2])
    energy = primitive[4] / (gamma_gas - 1.0) + kinetic
    return jnp.concatenate([density[None], density[None] * velocity, energy[None], density[None] * primitive[5:14]], axis=0)

def face_flux(lower_cells, upper_cells, direction):
    sides_data = []
    for side_cells in (lower_cells, upper_cells):
        amounts = conserved(side_cells)
        normal = side_cells[1 + direction]
        carried = amounts * normal[None]
        carried = carried.at[1 + direction].add(side_cells[4])
        carried = carried.at[4].add(side_cells[4] * normal)
        signal = jnp.abs(normal) + jnp.sqrt(gamma_gas * side_cells[4] / side_cells[0])
        sides_data.append((amounts, carried, signal))
    wave_speed = jnp.maximum(sides_data[0][2], sides_data[1][2])
    return 0.5 * (sides_data[0][1] + sides_data[1][1]) - 0.5 * wave_speed[None] * (sides_data[1][0] - sides_data[0][0])

def window(padded, array_axis, offset, extent):
    selection = [slice(None), slice(1, -1), slice(1, -1), slice(1, -1)]
    selection[array_axis] = slice(offset, offset + extent)
    return padded[tuple(selection)]

def advance(padded):
    primitive = padded[0:14]
    current = conserved(primitive[:, 1:-1, 1:-1, 1:-1])
    change = jnp.zeros_like(current)
    accelerations = []
    for direction in range(3):
        array_axis = 1 + direction
        extent = current.shape[array_axis]
        across = face_flux(window(primitive, array_axis, 0, extent + 1), window(primitive, array_axis, 1, extent + 1), direction)
        change = change + (lax.slice_in_dim(across, 1, extent + 1, axis=array_axis) - lax.slice_in_dim(across, 0, extent, axis=array_axis))
        accelerations.append(-0.5 * (window(padded[14:15], array_axis, 2, extent) - window(padded[14:15], array_axis, 0, extent))[0])
    updated = current - time_step * change
    density = current[0]
    momentum = jnp.concatenate([(updated[1 + direction] + time_step * density * accelerations[direction])[None] for direction in range(3)], axis=0)
    energy = updated[4] + time_step * (current[1] * accelerations[0] + current[2] * accelerations[1] + current[3] * accelerations[2])
    return (updated[0], momentum, energy, updated[5:14])

def eigenvalues(extent):
    waves = jnp.arange(extent).astype(jnp.float32)
    return 2.0 * jnp.cos(2.0 * jnp.pi / extent * waves) - 2.0

def solve_potential(density):
    total = eigenvalues(NX)[:, None, None] + eigenvalues(NY)[None, :, None] + eigenvalues(NZ)[None, None, :]
    green = jnp.where(total < 0.0, 1.0 / jnp.where(total < 0.0, total, -1.0), 0.0)
    return jnp.fft.ifftn(jnp.fft.fftn(density) * green).real

def reference(density, velocity, pressure, species, newton_count):
    potential = solve_potential(density)

    def one_block(block_number):
        rows_taken = (block_number * BX - 1 + jnp.arange(BX + 2, dtype=jnp.int32)) % NX

        def take_rows(field):
            return jnp.take(field, rows_taken, axis=field.ndim - 3)
        density_rows = take_rows(density)
        species_rows = take_rows(species)
        cooled = cooled_pressure(density_rows, take_rows(pressure), species_rows, take_rows(newton_count))
        gas_stack = jnp.concatenate([density_rows[None], take_rows(velocity), cooled[None], species_rows, take_rows(potential)[None]], axis=0)
        padded = jnp.pad(gas_stack, ((0, 0), (0, 0), (1, 1), (1, 1)), mode='wrap')
        return advance(padded)
    results = lax.map(one_block, jnp.arange(N_HX, dtype=jnp.int32))
    new_density = results[0].reshape(NX, NY, NZ)
    momentum = jnp.moveaxis(results[1], 1, 0).reshape(3, NX, NY, NZ)
    total_energy = results[2].reshape(NX, NY, NZ)
    species_mass = jnp.moveaxis(results[3], 1, 0).reshape(9, NX, NY, NZ)
    return (new_density, momentum, total_energy, species_mass, potential)
```

```python
import functools

import jax
import jax.numpy as jnp
import ml_dtypes
import numpy as np
from jax import lax
from jax.experimental import pallas as pl
from jax.experimental.pallas import tpu as pltpu
from jax.sharding import PartitionSpec as P

NEWTON = 4
gamma_gas = 5.0 / 3.0
time_step = 0.1
half_step = 0.5 * time_step
cool_rates = (2.0, 5.0, 9.0, 14.0, 20.0, 3.0, 7.0, 11.0, 29.0)
NX, NY, NZ = 128, 256, 256
BX, BY, BZ = 8, 32, 128
MESH = pl.DeviceIdType.MESH
f32 = jnp.float32
bf16 = jnp.bfloat16


def cas_table(length):
    keys = np.arange(length)
    angle = 2.0 * np.pi / length * (keys[:, None] * keys[None, :] % length)
    return np.cos(angle) + np.sin(angle)


def halves(table):
    table = table.astype(np.float32)
    high = table.astype(ml_dtypes.bfloat16)
    low = (table - high.astype(np.float32)).astype(ml_dtypes.bfloat16)
    return np.stack([high, low])


def eigen(extent):
    waves = np.arange(extent).astype(np.float32)
    return np.float32(2.0) * np.cos(np.float32(2.0 * np.pi / extent) * waves) - np.float32(2.0)


def tables():
    table_y = cas_table(NY)
    table_z = cas_table(NZ)
    parts = []
    for rank in range(NZ // BZ):
        first = rank * BZ
        edges = np.zeros((NZ, BZ))
        edges[:, 0] = table_z[:, (first - 1) % NZ]
        edges[:, BZ - 1] = table_z[:, (first + BZ) % NZ]
        parts.append(halves(np.concatenate([table_z[:, first : first + BZ], edges], axis=1)))
    lam_xy = (eigen(NX)[:, None] + eigen(NY)[None, :]).astype(np.float32)
    return np.stack(parts), halves(table_y), halves(cas_table(NX)), lam_xy, eigen(NZ).astype(np.float32)


def split(values):
    high = values.astype(bf16)
    return high, (values - high.astype(f32)).astype(bf16)


def dot3(left, right, dims=(((1,), (0,)), ((), ()))):
    def one(i, j):
        return lax.dot_general(left[i], right[j], dims, preferred_element_type=f32)

    return one(0, 0) + (one(0, 1) + one(1, 0))


def swap_chunks(tiles, lane):
    low = lane < 64
    even = (lane // 32) % 2 == 0
    mid = [None] * 4
    for i in range(2):
        mid[i] = jnp.where(low, tiles[i], pltpu.roll(tiles[i + 2], 64, 1))
        mid[i + 2] = jnp.where(low, pltpu.roll(tiles[i], 64, 1), tiles[i + 2])
    out = [None] * 4
    for i in (0, 2):
        out[i] = jnp.where(even, mid[i], pltpu.roll(mid[i + 1], 32, 1))
        out[i + 1] = jnp.where(even, pltpu.roll(mid[i], 96, 1), mid[i + 1])
    return out


def kernel(
    density, velocity, pressure, species, counts, tz_in, ty_in, tx_in, lam_in, lamz,
    o_density, o_momentum, o_energy, o_species, o_potential,
    gas, sound, press, count, tz, ty, tx, lam, out, pot,
    z_src, z_buf, u_buf, y_src, x_buf, x_src, w_buf, v_buf, b_src, b_buf,
    yp_src, yp_buf, zp_src, zp_buf, py_src, py_buf,
    in_sem, out_sem, send_sem, recv_sem, halo_send, halo_recv,
):
    a = lax.axis_index("hx")
    b = lax.axis_index("hy")
    g = lax.axis_index("ga")
    q = g * 8 + b

    loads = [
        (density, gas.at[0, pl.ds(1, BX)]),
        (tz_in.at[g], tz),
        (velocity, gas.at[pl.ds(1, 3), pl.ds(1, BX)]),
        (species, gas.at[pl.ds(5, 9), pl.ds(1, BX)]),
        (pressure, press),
        (counts, count),
        (ty_in, ty),
        (tx_in, tx),
        (lam_in, lam),
    ]
    loads = [pltpu.make_async_copy(s, d, in_sem.at[i]) for i, (s, d) in enumerate(loads)]
    for load in loads:
        load.start()

    barrier = pltpu.get_barrier_semaphore()

    def plane_id(offset):
        t = lax.rem(q + offset, 16)
        return t, {"hy": lax.rem(t, 8), "ga": t // 8}

    def line_id(offset):
        t = lax.rem(a + offset, 16)
        return t, {"hx": t}

    @pl.loop(1, 16)
    def _(d):
        pl.semaphore_signal(barrier, inc=1, device_id=plane_id(d)[1], device_id_type=MESH)
        pl.semaphore_signal(barrier, inc=1, device_id=line_id(d)[1], device_id_type=MESH)

    def remote(src, dst, sems, slot, target):
        return pltpu.make_async_remote_copy(
            src_ref=src, dst_ref=dst, send_sem=sems[0].at[slot], recv_sem=sems[1].at[slot],
            device_id=target, device_id_type=MESH,
        )

    rounds = [(send_sem.at[r], recv_sem.at[r]) for r in range(4)]

    def send1(d):
        t, where = plane_id(d)
        return remote(z_src.at[:, pl.ds(t * 16, 16)], z_buf.at[q], rounds[0], d, where)

    def send2(d):
        t, where = line_id(d)
        return remote(y_src.at[pl.ds(t * 8, 8)], x_buf.at[pl.ds(a * 8, 8)], rounds[1], d, where)

    def send3(d):
        t, where = line_id(d)
        return remote(x_src.at[pl.ds(t * 8, 8)], w_buf.at[pl.ds(a * 8, 8)], rounds[2], d, where)

    def send4(d):
        t, where = plane_id(d)
        return remote(b_src.at[lax.rem(t, 8)], b_buf.at[:, pl.ds(q * 16, 16)], rounds[3], d, where)

    def start_all(send):
        @pl.loop(1, 16)
        def _(d):
            send(d).start()

    def arrive_all(send):
        @pl.loop(1, 16)
        def _(d):
            send(d).wait_recv()

    lane16 = lax.broadcasted_iota(jnp.int32, (16, 128), 1)

    loads[0].wait()
    loads[1].wait()
    brick = split(gas[0, pl.ds(1, BX)].reshape(BX * BY, BZ) - 1.0)
    turned = dot3((tz[0, :, 0:BZ], tz[1, :, 0:BZ]), brick, (((1,), (1,)), ((), ())))
    z_src[0] = turned[:, 0:128]
    z_src[1] = turned[:, 128:256]
    pl.semaphore_wait(barrier, 30)
    start_all(send1)
    z_buf[q] = z_src[:, pl.ds(pl.multiple_of(q * 16, 16), 16)]

    halos = (halo_send, halo_recv)
    above = {"hx": lax.rem(a + 1, 16)}
    below = {"hx": lax.rem(a + 15, 16)}
    right = {"hy": lax.rem(b + 1, 8)}
    left = {"hy": lax.rem(b + 7, 8)}
    other = {"ga": 1 - g}
    loads[2].wait()
    loads[3].wait()
    face_early = []
    for slot, (first, many) in enumerate(((0, 4), (5, 9))):
        rows = pl.ds(first, many)
        face_early.append(remote(gas.at[rows, BX], gas.at[rows, 0], halos, 2 * slot, above))
        face_early.append(remote(gas.at[rows, 1], gas.at[rows, BX + 1], halos, 2 * slot + 1, below))
    for face in face_early:
        face.start()
    loads[4].wait()
    loads[5].wait()
    lane8 = lax.broadcasted_iota(jnp.int32, (8, 128), 1)

    def cell_sound(p):
        return jnp.sqrt(gamma_gas * gas[4, p] / gas[0, p])

    @pl.loop(0, BX)
    def _(i):
        p = i + 1
        rho = gas[0, p]
        cooling = cool_rates[0] * gas[5, p]
        for s in range(1, 9):
            cooling = cooling + cool_rates[s] * gas[5 + s, p]
        stiffness = time_step * rho * cooling
        initial = press[i] / ((gamma_gas - 1.0) * rho)
        many = count[i]
        energy = initial
        for step in range(NEWTON):
            near = 1.0 + energy
            square = near * near
            top = (energy - initial) * square + stiffness * energy * energy * near
            bottom = square + stiffness * energy * (energy + 2.0)
            energy = jnp.where(many > step, energy - top / bottom, energy)
        gas[4, p] = (gamma_gas - 1.0) * rho * energy
        sound[p] = jnp.sqrt(gamma_gas * (gamma_gas - 1.0) * energy)
        tile = jnp.zeros((8, 128), f32)
        for f in range(15):
            field = gas[f, p] if f < 14 else sound[p]
            yp_src[0, i, f : f + 1, :] = field[BY - 1 : BY]
            yp_src[1, i, f : f + 1, :] = field[0:1]
            for j in range(4):
                moved = pltpu.roll(field[8 * j : 8 * j + 8], 32 * j + 2 * f + 1, 1)
                tile = jnp.where(lane8 // 2 == 16 * j + f, moved, tile)
        zp_src[i] = tile
        yp_src[0, i, 15:16, :] = jnp.zeros((1, 128), f32)
        yp_src[1, i, 15:16, :] = jnp.zeros((1, 128), f32)

    face_late = [
        remote(yp_src.at[0], yp_buf.at[0], halos, 6, right),
        remote(yp_src.at[1], yp_buf.at[1], halos, 7, left),
        remote(zp_src, zp_buf, halos, 8, other),
        remote(gas.at[4, BX], gas.at[4, 0], halos, 4, above),
        remote(gas.at[4, 1], gas.at[4, BX + 1], halos, 5, below),
    ]
    for face in face_late:
        face.start()

    loads[8].wait()
    total = lam[...] + lamz[q * 16 + a]
    inside = total < 0.0
    lam[...] = jnp.where(inside, (1.0 / (NX * NY * NZ)) / jnp.where(inside, total, -1.0), 0.0)

    row32 = lax.broadcasted_iota(jnp.int32, (BY, BZ), 0)
    lane32 = lax.broadcasted_iota(jnp.int32, (BY, BZ), 1)

    def hydro(i):
        p = i + 1

        def at(f, where):
            return gas[f, where] if f < 14 else sound[where]

        def sides(f, d):
            if d == 0:
                return at(f, p - 1), at(f, p + 1)
            field = at(f, p)
            if d == 1:
                lower = jnp.where(row32 == 0, yp_buf[0, i, f : f + 1, :], pltpu.roll(field, 1, 0))
                upper = jnp.where(
                    row32 == BY - 1, yp_buf[1, i, f : f + 1, :], pltpu.roll(field, BY - 1, 0)
                )
                return lower, upper
            tile = zp_buf[i]
            edge = jnp.concatenate(
                [pltpu.roll(tile, (BZ - 1 - 32 * j - 2 * f) % 128, 1) for j in range(4)], axis=0
            )
            lower = pltpu.roll(jnp.where(lane32 == BZ - 1, edge, field), 1, 1)
            upper = pltpu.roll(jnp.where(lane32 == 0, edge, field), BZ - 1, 1)
            return lower, upper

        rho = gas[0, p]
        vel = [gas[1 + k, p] for k in range(3)]
        cs = sound[p]
        keep = 1.0
        weights = []
        new_rho = 0.0
        new_energy = 0.0
        new_mom = [0.0, 0.0, 0.0]
        for d in range(3):
            rho_l, rho_u = sides(0, d)
            v_l, v_u = zip(*[sides(1 + k, d) for k in range(3)])
            p_l, p_u = sides(4, d)
            c_l, c_u = sides(14, d)
            here = jnp.abs(vel[d]) + cs
            w_l = jnp.maximum(here, jnp.abs(v_l[d]) + c_l)
            w_u = jnp.maximum(here, jnp.abs(v_u[d]) + c_u)
            b_l = half_step * (w_l + v_l[d])
            b_u = half_step * (w_u - v_u[d])
            a_l = b_l * rho_l
            a_u = b_u * rho_u
            keep = keep - half_step * (w_l + w_u)
            weights.append((a_l, a_u))
            new_rho = new_rho + (a_l + a_u)
            for k in range(3):
                new_mom[k] = new_mom[k] + (a_l * v_l[k] + a_u * v_u[k])
            new_mom[d] = new_mom[d] + half_step * (p_l - p_u)
            sq_l = v_l[0] * v_l[0] + v_l[1] * v_l[1] + v_l[2] * v_l[2]
            sq_u = v_u[0] * v_u[0] + v_u[1] * v_u[1] + v_u[2] * v_u[2]
            new_energy = new_energy + (
                0.5 * (a_l * sq_l + a_u * sq_u)
                + p_l * (1.5 * b_l + half_step * v_l[d])
                + p_u * (1.5 * b_u - half_step * v_u[d])
            )
        mass = keep * rho
        out[0, i] = new_rho + mass
        for k in range(3):
            out[1 + k, i] = new_mom[k] + mass * vel[k]
        sq = vel[0] * vel[0] + vel[1] * vel[1] + vel[2] * vel[2]
        out[4, i] = new_energy + keep * (1.5 * gas[4, p]) + 0.5 * mass * sq
        for s in range(5, 14):
            result = mass * gas[s, p]
            for d in range(3):
                lower, upper = sides(s, d)
                result = result + (weights[d][0] * lower + weights[d][1] * upper)
            out[s, i] = result

    loads[6].wait()
    arrive_all(send1)
    for hi in range(2):
        for xh in range(2):
            tiles = [z_buf[4 * hi + i, xh] + z_buf[8 + 4 * hi + i, xh] for i in range(4)]
            tiles = swap_chunks(tiles, lane16)
            for xl in range(4):
                u_buf[hi, pl.ds(4 * xh + xl, 16, stride=8), :] = tiles[xl]
    lines = split(jnp.concatenate([u_buf[0], u_buf[1]], axis=1))
    table_y = (ty[0], ty[1])
    y_src[...] = dot3(lines, table_y)
    start_all(send2)
    x_buf[pl.ds(pl.multiple_of(a * 8, 8), 8)] = y_src[pl.ds(pl.multiple_of(a * 8, 8), 8)]

    for face in face_late[0:3]:
        face.wait_recv()

    @pl.loop(1, 4)
    def _(i):
        hydro(i)

    loads[7].wait()
    arrive_all(send2)
    table_x = (tx[0], tx[1])
    waves = dot3(table_x, split(x_buf[...])) * lam[...]
    x_src[...] = dot3(table_x, split(waves))
    start_all(send3)
    w_buf[pl.ds(pl.multiple_of(a * 8, 8), 8)] = x_src[pl.ds(pl.multiple_of(a * 8, 8), 8)]

    @pl.loop(4, 7)
    def _(i):
        hydro(i)

    arrive_all(send3)
    back = dot3(split(w_buf[...]), table_y)
    v_buf[0] = back[:, 0:128]
    v_buf[1] = back[:, 128:256]
    for hi in range(2):
        for xh in range(2):
            tiles = [v_buf[hi, pl.ds(4 * xh + xl, 16, stride=8), :] for xl in range(4)]
            tiles = swap_chunks(tiles, lane16)
            for i in range(4):
                b_src[4 * hi + i, xh] = tiles[i]
    start_all(send4)
    b_buf[:, pl.ds(pl.multiple_of(q * 16, 16), 16)] = b_src[b]

    for face in face_early + face_late[3:5]:
        face.wait_recv()
    sound[0] = cell_sound(0)
    sound[BX + 1] = cell_sound(BX + 1)

    @pl.loop(0, 2)
    def _(i):
        hydro(i * (BX - 1))

    stores = [
        pltpu.make_async_copy(out.at[0], o_density, out_sem.at[0]),
        pltpu.make_async_copy(out.at[pl.ds(5, 9)], o_species, out_sem.at[1]),
    ]
    stores[0].start()
    stores[1].start()

    arrive_all(send4)
    table_back = (tz[0], tz[1])
    edges = []
    for xh in range(2):
        done = dot3(split(b_buf[xh].T), table_back)
        edges.append(done[:, BZ:])
        for xl in range(4):
            x = 4 * xh + xl
            pot[1 + x] = done[32 * xl : 32 * xl + 32, 0:BZ]
            py_src[0, x : x + 1, :] = done[32 * xl + 31 : 32 * xl + 32, 0:BZ]
            py_src[1, x : x + 1, :] = done[32 * xl : 32 * xl + 1, 0:BZ]
    pot_faces = [
        remote(pot.at[BX], pot.at[0], halos, 9, above),
        remote(pot.at[1], pot.at[BX + 1], halos, 10, below),
        remote(py_src.at[0], py_buf.at[0], halos, 11, right),
        remote(py_src.at[1], py_buf.at[1], halos, 12, left),
    ]
    for face in pot_faces:
        face.start()
    stores.append(pltpu.make_async_copy(pot.at[pl.ds(1, BX)], o_potential, out_sem.at[2]))
    stores[2].start()
    for face in pot_faces:
        face.wait_recv()
    for i in range(BX):
        here = pot[1 + i]
        edge = edges[i // 4][32 * (i % 4) : 32 * (i % 4) + 32]
        pull = [
            pot[i] - pot[i + 2],
            jnp.where(row32 == 0, py_buf[0, i : i + 1, :], pltpu.roll(here, 1, 0))
            - jnp.where(row32 == BY - 1, py_buf[1, i : i + 1, :], pltpu.roll(here, BY - 1, 0)),
            jnp.where(lane32 == 0, edge, pltpu.roll(here, 1, 1))
            - jnp.where(lane32 == BZ - 1, edge, pltpu.roll(here, BZ - 1, 1)),
        ]
        weight = half_step * gas[0, 1 + i]
        work = out[4, i]
        for k in range(3):
            push = weight * pull[k]
            out[1 + k, i] = out[1 + k, i] + push
            work = work + push * gas[1 + k, 1 + i]
        out[4, i] = work
    stores.append(pltpu.make_async_copy(out.at[pl.ds(1, 3)], o_momentum, out_sem.at[3]))
    stores.append(pltpu.make_async_copy(out.at[4], o_energy, out_sem.at[4]))
    stores[3].start()
    stores[4].start()

    for send in (send1, send2, send3, send4):

        @pl.loop(1, 16)
        def _(d):
            send(d).wait_send()

    for face in face_early + face_late + pot_faces:
        face.wait_send()
    for store in stores:
        store.wait()


def local(density, velocity, pressure, species, counts):
    brick = (BX, BY, BZ)
    shape = jax.ShapeDtypeStruct
    anywhere = pl.BlockSpec(memory_space=pl.ANY)
    vmem = pltpu.VMEM
    table_z, table_y, table_x, lam_xy, lam_z = tables()
    return pl.pallas_call(
        kernel,
        out_shape=(
            shape(brick, f32),
            shape((3,) + brick, f32),
            shape(brick, f32),
            shape((9,) + brick, f32),
            shape(brick, f32),
        ),
        in_specs=[anywhere] * 9 + [pl.BlockSpec(memory_space=pltpu.SMEM)],
        out_specs=(anywhere,) * 5,
        scratch_shapes=[
            vmem((14, BX + 2, BY, BZ), f32),
            vmem((BX + 2, BY, BZ), f32),
            vmem(brick, f32),
            vmem(brick, jnp.int32),
            vmem((2, NZ, 2 * BZ), bf16),
            vmem((2, NY, NY), bf16),
            vmem((2, NX, NX), bf16),
            vmem((NX, NY), f32),
            vmem((14,) + brick, f32),
            vmem((BX + 2, BY, BZ), f32),
            vmem((2, NZ, 128), f32),
            vmem((16, 2, 16, 128), f32),
            vmem((2, 128, 128), f32),
            vmem((128, 256), f32),
            vmem((128, 256), f32),
            vmem((128, 256), f32),
            vmem((128, 256), f32),
            vmem((2, 128, 128), f32),
            vmem((8, 2, 16, 128), f32),
            vmem((2, NZ, 128), f32),
            vmem((2, BX, 16, BZ), f32),
            vmem((2, BX, 16, BZ), f32),
            vmem((BX, 8, 128), f32),
            vmem((BX, 8, 128), f32),
            vmem((2, BX, BZ), f32),
            vmem((2, BX, BZ), f32),
            pltpu.SemaphoreType.DMA((9,)),
            pltpu.SemaphoreType.DMA((5,)),
            pltpu.SemaphoreType.DMA((4, 16)),
            pltpu.SemaphoreType.DMA((4, 16)),
            pltpu.SemaphoreType.DMA((13,)),
            pltpu.SemaphoreType.DMA((13,)),
        ],
        compiler_params=pltpu.CompilerParams(
            collective_id=0, has_side_effects=True, vmem_limit_bytes=40 * 1024 * 1024
        ),
        name="step",
    )(density, velocity, pressure, species, counts, table_z, table_y, table_x, lam_xy, lam_z)


def solution(mesh):
    in_specs = (
        P("hx", "hy", "ga"),
        P(None, "hx", "hy", "ga"),
        P("hx", "hy", "ga"),
        P(None, "hx", "hy", "ga"),
        P("hx", "hy", "ga"),
    )
    out_specs = (
        P("hx", "hy", "ga"),
        P(None, "hx", "hy", "ga"),
        P("hx", "hy", "ga"),
        P(None, "hx", "hy", "ga"),
        P("hx", "hy", "ga"),
    )
    return jax.shard_map(local, mesh=mesh, in_specs=in_specs, out_specs=out_specs, check_vma=False)
```

```python
import functools

import jax
import jax.numpy as jnp
import ml_dtypes
import numpy as np
from jax import lax
from jax.experimental import pallas as pl
from jax.experimental.pallas import tpu as pltpu
from jax.sharding import PartitionSpec as P

NEWTON = 4
gamma_gas = 5.0 / 3.0
time_step = 0.1
half_step = 0.5 * time_step
cool_rates = (2.0, 5.0, 9.0, 14.0, 20.0, 3.0, 7.0, 11.0, 29.0)
NX, NY, NZ = 128, 256, 256
BX, BY, BZ = 8, 32, 128
MESH = pl.DeviceIdType.MESH
f32 = jnp.float32
bf16 = jnp.bfloat16


def cas_table(length):
    keys = np.arange(length)
    angle = 2.0 * np.pi / length * (keys[:, None] * keys[None, :] % length)
    return np.cos(angle) + np.sin(angle)


def halves(table):
    table = table.astype(np.float32)
    high = table.astype(ml_dtypes.bfloat16)
    low = (table - high.astype(np.float32)).astype(ml_dtypes.bfloat16)
    return np.stack([high, low])


def eigen(extent):
    waves = np.arange(extent).astype(np.float32)
    return np.float32(2.0) * np.cos(np.float32(2.0 * np.pi / extent) * waves) - np.float32(2.0)


def tables():
    table_y = cas_table(NY)
    table_z = cas_table(NZ)
    parts = []
    for rank in range(NZ // BZ):
        first = rank * BZ
        edges = np.zeros((NZ, BZ))
        edges[:, 0] = table_z[:, (first - 1) % NZ]
        edges[:, BZ - 1] = table_z[:, (first + BZ) % NZ]
        parts.append(halves(np.concatenate([table_z[:, first : first + BZ], edges], axis=1)))
    lam_xy = (eigen(NX)[:, None] + eigen(NY)[None, :]).astype(np.float32)
    table_x = cas_table(NX)
    beyond = np.zeros((NX // BX, 8, NX))
    for block in range(NX // BX):
        beyond[block, 0:4:2] = table_x[(block * BX - 1) % NX]
        beyond[block, 1:4:2] = table_x[(block * BX + BX) % NX]
    table_x = np.concatenate([table_x, beyond.reshape(NX, NX)])
    return np.stack(parts), halves(table_y), halves(table_x), lam_xy, eigen(NZ).astype(np.float32)


def split(values):
    high = values.astype(bf16)
    return high, (values - high.astype(f32)).astype(bf16)


def dot3(left, right, dims=(((1,), (0,)), ((), ()))):
    def one(i, j):
        return lax.dot_general(left[i], right[j], dims, preferred_element_type=f32)

    return one(0, 0) + (one(0, 1) + one(1, 0))


def swap_chunks(tiles, lane):
    low = lane < 64
    even = (lane // 32) % 2 == 0
    mid = [None] * 4
    for i in range(2):
        mid[i] = jnp.where(low, tiles[i], pltpu.roll(tiles[i + 2], 64, 1))
        mid[i + 2] = jnp.where(low, pltpu.roll(tiles[i], 64, 1), tiles[i + 2])
    out = [None] * 4
    for i in (0, 2):
        out[i] = jnp.where(even, mid[i], pltpu.roll(mid[i + 1], 32, 1))
        out[i + 1] = jnp.where(even, pltpu.roll(mid[i], 96, 1), mid[i + 1])
    return out


def kernel(
    density, velocity, pressure, species, counts, tz_in, ty_in, tx_in, lam_in, lamz,
    o_density, o_momentum, o_energy, o_species, b_buf,
    gas, sound, press, count, tz, ty, tx, lam, out,
    z_src, z_buf, u_buf, y_src, x_buf, x_src, w_buf, v_buf, b_src,
    yp_src, yp_buf, zp_src, zp_buf,
    in_sem, out_sem, send_sem, recv_sem, halo_send, halo_recv,
):
    a = lax.axis_index("hx")
    b = lax.axis_index("hy")
    g = lax.axis_index("ga")
    q = g * 8 + b
    side = lax.rem(g + a, 2)
    chunk = side * 8 + b

    loads = [
        (density, gas.at[0, pl.ds(1, BX)]),
        (tz_in.at[g], tz),
        (velocity, gas.at[pl.ds(1, 3), pl.ds(1, BX)]),
        (species, gas.at[pl.ds(5, 9), pl.ds(1, BX)]),
        (pressure, press),
        (counts, count),
        (ty_in, ty),
        (tx_in, tx),
        (lam_in, lam),
    ]
    loads = [pltpu.make_async_copy(s, d, in_sem.at[i]) for i, (s, d) in enumerate(loads)]
    for load in loads:
        load.start()

    barrier = pltpu.get_barrier_semaphore()

    def outward(n, middle):
        return middle + ((n + 1) // 2) * (2 * lax.rem(n, 2) - 1)

    def plane_id(n):
        t_b = lax.rem(b + outward(n // 2, 4), 8)
        t_g = lax.rem(g + 1 + n, 2)
        return t_b, t_g, {"hy": t_b, "ga": t_g}

    def line_id(n):
        t = lax.rem(a + outward(n, 8), 16)
        return t, {"hx": t, "ga": lax.rem(side + t, 2)}

    above = {"hx": lax.rem(a + 1, 16)}
    below = {"hx": lax.rem(a + 15, 16)}

    @pl.loop(0, 15)
    def _(n):
        pl.semaphore_signal(barrier, inc=1, device_id=plane_id(n)[2], device_id_type=MESH)
        pl.semaphore_signal(barrier, inc=1, device_id=line_id(n)[1], device_id_type=MESH)

    pl.semaphore_signal(barrier, inc=1, device_id=above, device_id_type=MESH)
    pl.semaphore_signal(barrier, inc=1, device_id=below, device_id_type=MESH)

    def remote(src, dst, sems, slot, target):
        return pltpu.make_async_remote_copy(
            src_ref=src, dst_ref=dst, send_sem=sems[0].at[slot], recv_sem=sems[1].at[slot],
            device_id=target, device_id_type=MESH,
        )

    rounds = [(send_sem.at[r], recv_sem.at[r]) for r in range(4)]

    def send1(n):
        t_b, t_g, where = plane_id(n)
        t = lax.rem(t_g + a, 2) * 8 + t_b
        return remote(z_src.at[:, pl.ds(t * 16, 16)], z_buf.at[q], rounds[0], n, where)

    def send2(n):
        t, where = line_id(n)
        return remote(y_src.at[pl.ds(t * 8, 8)], x_buf.at[pl.ds(a * 8, 8)], rounds[1], n, where)

    def send3(n):
        t, where = line_id(n)
        return remote(x_src.at[pl.ds(t * 8, 8)], w_buf.at[pl.ds(a * 8, 8)], rounds[2], n, where)

    def send4(n):
        t_b, _, where = plane_id(n)
        return remote(b_src.at[t_b], b_buf.at[:, pl.ds(chunk * 16, 16)], rounds[3], n, where)

    def start_all(send):
        @pl.loop(0, 15)
        def _(n):
            send(n).start()

    def arrive_all(send):
        @pl.loop(0, 15)
        def _(n):
            send(n).wait_recv()

    lane16 = lax.broadcasted_iota(jnp.int32, (16, 128), 1)

    loads[0].wait()
    loads[1].wait()
    brick = split(gas[0, pl.ds(1, BX)].reshape(BX * BY, BZ) - 1.0)
    turned = dot3((tz[0, :, 0:BZ], tz[1, :, 0:BZ]), brick, (((1,), (1,)), ((), ())))
    z_src[0] = turned[:, 0:128]
    z_src[1] = turned[:, 128:256]
    pl.semaphore_wait(barrier, 32)
    start_all(send1)
    z_buf[q] = z_src[:, pl.ds(pl.multiple_of(chunk * 16, 16), 16)]

    halos = (halo_send, halo_recv)
    right = {"hy": lax.rem(b + 1, 8)}
    left = {"hy": lax.rem(b + 7, 8)}
    other = {"ga": 1 - g}
    loads[2].wait()
    loads[3].wait()
    face_early = []
    for slot, (first, many) in enumerate(((0, 4), (5, 9))):
        rows = pl.ds(first, many)
        face_early.append(remote(gas.at[rows, BX], gas.at[rows, 0], halos, 2 * slot, above))
        face_early.append(remote(gas.at[rows, 1], gas.at[rows, BX + 1], halos, 2 * slot + 1, below))
    for face in face_early:
        face.start()
    loads[4].wait()
    loads[5].wait()
    lane8 = lax.broadcasted_iota(jnp.int32, (8, 128), 1)

    def cell_sound(p):
        return jnp.sqrt(gamma_gas * gas[4, p] / gas[0, p])

    @pl.loop(0, BX)
    def _(i):
        p = i + 1
        rho = gas[0, p]
        cooling = cool_rates[0] * gas[5, p]
        for s in range(1, 9):
            cooling = cooling + cool_rates[s] * gas[5 + s, p]
        stiffness = time_step * rho * cooling
        initial = press[i] / ((gamma_gas - 1.0) * rho)
        many = count[i]
        energy = initial
        for step in range(NEWTON):
            near = 1.0 + energy
            square = near * near
            top = (energy - initial) * square + stiffness * energy * energy * near
            bottom = square + stiffness * energy * (energy + 2.0)
            energy = jnp.where(many > step, energy - top / bottom, energy)
        gas[4, p] = (gamma_gas - 1.0) * rho * energy
        sound[p] = jnp.sqrt(gamma_gas * (gamma_gas - 1.0) * energy)
        tile = jnp.zeros((8, 128), f32)
        for f in range(15):
            field = gas[f, p] if f < 14 else sound[p]
            yp_src[0, i, f : f + 1, :] = field[BY - 1 : BY]
            yp_src[1, i, f : f + 1, :] = field[0:1]
            for j in range(4):
                moved = pltpu.roll(field[8 * j : 8 * j + 8], 32 * j + 2 * f + 1, 1)
                tile = jnp.where(lane8 // 2 == 16 * j + f, moved, tile)
        zp_src[i] = tile
        yp_src[0, i, 15:16, :] = jnp.zeros((1, 128), f32)
        yp_src[1, i, 15:16, :] = jnp.zeros((1, 128), f32)

    face_late = [
        remote(yp_src.at[0], yp_buf.at[0], halos, 6, right),
        remote(yp_src.at[1], yp_buf.at[1], halos, 7, left),
        remote(zp_src, zp_buf, halos, 8, other),
        remote(gas.at[4, BX], gas.at[4, 0], halos, 4, above),
        remote(gas.at[4, 1], gas.at[4, BX + 1], halos, 5, below),
    ]
    for face in face_late:
        face.start()

    loads[8].wait()
    total = lam[...] + lamz[chunk * 16 + a]
    inside = total < 0.0
    lam[...] = jnp.where(inside, (1.0 / (NX * NY * NZ)) / jnp.where(inside, total, -1.0), 0.0)

    row32 = lax.broadcasted_iota(jnp.int32, (BY, BZ), 0)
    lane32 = lax.broadcasted_iota(jnp.int32, (BY, BZ), 1)

    def hydro(i):
        p = i + 1

        def at(f, where):
            return gas[f, where] if f < 14 else sound[where]

        def sides(f, d):
            if d == 0:
                return at(f, p - 1), at(f, p + 1)
            field = at(f, p)
            if d == 1:
                lower = jnp.where(row32 == 0, yp_buf[0, i, f : f + 1, :], pltpu.roll(field, 1, 0))
                upper = jnp.where(
                    row32 == BY - 1, yp_buf[1, i, f : f + 1, :], pltpu.roll(field, BY - 1, 0)
                )
                return lower, upper
            tile = zp_buf[i]
            edge = jnp.concatenate(
                [pltpu.roll(tile, (BZ - 1 - 32 * j - 2 * f) % 128, 1) for j in range(4)], axis=0
            )
            lower = pltpu.roll(jnp.where(lane32 == BZ - 1, edge, field), 1, 1)
            upper = pltpu.roll(jnp.where(lane32 == 0, edge, field), BZ - 1, 1)
            return lower, upper

        rho = gas[0, p]
        vel = [gas[1 + k, p] for k in range(3)]
        cs = sound[p]
        keep = 1.0
        weights = []
        new_rho = 0.0
        new_energy = 0.0
        new_mom = [0.0, 0.0, 0.0]
        for d in range(3):
            rho_l, rho_u = sides(0, d)
            v_l, v_u = zip(*[sides(1 + k, d) for k in range(3)])
            p_l, p_u = sides(4, d)
            c_l, c_u = sides(14, d)
            here = jnp.abs(vel[d]) + cs
            w_l = jnp.maximum(here, jnp.abs(v_l[d]) + c_l)
            w_u = jnp.maximum(here, jnp.abs(v_u[d]) + c_u)
            b_l = half_step * (w_l + v_l[d])
            b_u = half_step * (w_u - v_u[d])
            a_l = b_l * rho_l
            a_u = b_u * rho_u
            keep = keep - half_step * (w_l + w_u)
            weights.append((a_l, a_u))
            new_rho = new_rho + (a_l + a_u)
            for k in range(3):
                new_mom[k] = new_mom[k] + (a_l * v_l[k] + a_u * v_u[k])
            new_mom[d] = new_mom[d] + half_step * (p_l - p_u)
            sq_l = v_l[0] * v_l[0] + v_l[1] * v_l[1] + v_l[2] * v_l[2]
            sq_u = v_u[0] * v_u[0] + v_u[1] * v_u[1] + v_u[2] * v_u[2]
            new_energy = new_energy + (
                0.5 * (a_l * sq_l + a_u * sq_u)
                + p_l * (1.5 * b_l + half_step * v_l[d])
                + p_u * (1.5 * b_u - half_step * v_u[d])
            )
        mass = keep * rho
        out[0, i] = new_rho + mass
        for k in range(3):
            out[1 + k, i] = new_mom[k] + mass * vel[k]
        sq = vel[0] * vel[0] + vel[1] * vel[1] + vel[2] * vel[2]
        out[4, i] = new_energy + keep * (1.5 * gas[4, p]) + 0.5 * mass * sq
        for s in range(5, 14):
            result = mass * gas[s, p]
            for d in range(3):
                lower, upper = sides(s, d)
                result = result + (weights[d][0] * lower + weights[d][1] * upper)
            out[s, i] = result

    loads[6].wait()
    arrive_all(send1)
    for hi in range(2):
        for xh in range(2):
            tiles = [z_buf[4 * hi + i, xh] + z_buf[8 + 4 * hi + i, xh] for i in range(4)]
            tiles = swap_chunks(tiles, lane16)
            for xl in range(4):
                u_buf[hi, pl.ds(4 * xh + xl, 16, stride=8), :] = tiles[xl]
    lines = split(jnp.concatenate([u_buf[0], u_buf[1]], axis=1))
    table_y = (ty[0], ty[1])
    y_src[...] = dot3(lines, table_y)
    start_all(send2)
    x_buf[pl.ds(pl.multiple_of(a * 8, 8), 8)] = y_src[pl.ds(pl.multiple_of(a * 8, 8), 8)]

    for face in face_late[0:3]:
        face.wait_recv()

    @pl.loop(1, 4)
    def _(i):
        hydro(i)

    loads[7].wait()
    arrive_all(send2)
    waves = dot3((tx[0, 0:NX], tx[1, 0:NX]), split(x_buf[...])) * lam[...]
    solved = dot3((tx[0], tx[1]), split(waves))
    x_src[:, 0:NY] = solved[0:NX]
    row128 = lax.broadcasted_iota(jnp.int32, (NX, 128), 0)
    x_src[:, NY:] = jnp.where(row128 % 8 < 2, solved[NX:, 0:128], solved[NX:, 128:NY])
    start_all(send3)
    w_buf[pl.ds(pl.multiple_of(a * 8, 8), 8)] = x_src[pl.ds(pl.multiple_of(a * 8, 8), 8)]

    @pl.loop(4, 7)
    def _(i):
        hydro(i)

    arrive_all(send3)
    faces = w_buf[:, NY:]
    faces = jnp.concatenate([faces, pltpu.roll(faces, NX - 2, 0)], axis=1)
    back = dot3(split(jnp.concatenate([w_buf[:, 0:NY], faces], axis=0)), table_y)
    for hi in range(2):
        v_buf[0, hi] = back[0:NX, 128 * hi : 128 * hi + 128]
        v_buf[1, hi] = back[NX:, 128 * hi : 128 * hi + 128]

    def line(kind, hi, row):
        return v_buf[kind, hi, pl.ds(row, 16, stride=8), :]

    spot = lane16 % 32
    for hi in range(2):
        rows_low = jnp.zeros((16, 128), f32)
        rows_high = rows_low
        for xh in range(2):
            tiles = [line(0, hi, 4 * xh + xl) for xl in range(4)]
            outer = [line(0, 1 - hi, 4 * xh + xl) for xl in range(4)]
            for xl in range(4):
                x = 4 * xh + xl
                low = jnp.where(
                    lane16 < 32, pltpu.roll(outer[xl], 1 + x, 1), pltpu.roll(tiles[xl], 1 + x, 1)
                )
                high = jnp.where(
                    lane16 >= 96, pltpu.roll(outer[xl], 96 + x, 1), pltpu.roll(tiles[xl], 96 + x, 1)
                )
                rows_low = jnp.where(spot == x, low, rows_low)
                rows_high = jnp.where(spot == x, high, rows_high)
            tiles = swap_chunks(tiles, lane16)
            for i in range(4):
                b_src[4 * hi + i, xh] = tiles[i]
        tiles = swap_chunks([line(1, hi, 0), line(1, hi, 1), rows_low, rows_high], lane16)
        for i in range(4):
            b_src[4 * hi + i, 2] = tiles[i]
    start_all(send4)
    own = pltpu.make_async_copy(b_src.at[b], b_buf.at[:, pl.ds(chunk * 16, 16)], out_sem.at[4])
    own.start()

    for face in face_early + face_late[3:5]:
        face.wait_recv()
    sound[0] = cell_sound(0)
    sound[BX + 1] = cell_sound(BX + 1)

    @pl.loop(0, 2)
    def _(i):
        hydro(i * (BX - 1))

    stores = [
        own,
        pltpu.make_async_copy(out.at[0], o_density, out_sem.at[0]),
        pltpu.make_async_copy(out.at[pl.ds(1, 3)], o_momentum, out_sem.at[1]),
        pltpu.make_async_copy(out.at[4], o_energy, out_sem.at[2]),
        pltpu.make_async_copy(out.at[pl.ds(5, 9)], o_species, out_sem.at[3]),
    ]
    for store in stores[1:]:
        store.start()

    for send in (send1, send2, send3, send4):

        @pl.loop(0, 15)
        def _(n):
            send(n).wait_send()

    for face in face_early + face_late:
        face.wait_send()
    for store in stores:
        store.wait()
    arrive_all(send4)


def finish(
    density, velocity, density_in, momentum_in, energy_in, species_in, waves, tz_in,
    o_density, o_momentum, o_energy, o_species, o_potential,
    rho, vel, new_rho, mom, energy, frac, spec, tz, pot, load_sem, store_sem,
):
    loads = [
        (waves, spec),
        (tz_in.at[lax.axis_index("ga")], tz),
        (density_in, new_rho),
        (species_in, frac),
        (density, rho),
        (velocity, vel),
        (momentum_in, mom),
        (energy_in, energy),
    ]
    loads = [pltpu.make_async_copy(s, d, load_sem.at[i]) for i, (s, d) in enumerate(loads)]
    stores = [
        (new_rho, o_density),
        (frac, o_species),
        (pot.at[pl.ds(1, BX)], o_potential),
        (mom, o_momentum),
        (energy, o_energy),
    ]
    stores = [pltpu.make_async_copy(s, d, store_sem.at[i]) for i, (s, d) in enumerate(stores)]
    for load in loads:
        load.start()
    loads[0].wait()
    loads[1].wait()
    table = (tz[0], tz[1])
    edges = []
    for xh in range(2):
        done = dot3(split(spec[xh].T), table)
        edges.append(done[:, BZ:])
        for xl in range(4):
            pot[1 + 4 * xh + xl] = done[32 * xl : 32 * xl + 32, 0:BZ]
    stores[2].start()
    done = dot3(split(spec[2].T), (tz[0, :, 0:BZ], tz[1, :, 0:BZ]))
    pot[0] = done[0:32]
    pot[BX + 1] = done[32:64]
    for i in range(2):
        loads[2 + i].wait()
        stores[i].start()
    for load in loads[4:]:
        load.wait()
    row32 = lax.broadcasted_iota(jnp.int32, (BY, BZ), 0)
    lane32 = lax.broadcasted_iota(jnp.int32, (BY, BZ), 1)
    for i in range(BX):
        here = pot[1 + i]
        edge = edges[i // 4][32 * (i % 4) : 32 * (i % 4) + 32]
        pull = [
            pot[i] - pot[i + 2],
            jnp.where(row32 == 0, done[64 + i : 65 + i], pltpu.roll(here, 1, 0))
            - jnp.where(row32 == BY - 1, done[96 + i : 97 + i], pltpu.roll(here, BY - 1, 0)),
            jnp.where(lane32 == 0, edge, pltpu.roll(here, 1, 1))
            - jnp.where(lane32 == BZ - 1, edge, pltpu.roll(here, BZ - 1, 1)),
        ]
        weight = half_step * rho[i]
        work = energy[i]
        for k in range(3):
            push = weight * pull[k]
            mom[k, i] = mom[k, i] + push
            work = work + push * vel[k, i]
        energy[i] = work
    stores[3].start()
    stores[4].start()
    for store in stores:
        store.wait()


def local(density, velocity, pressure, species, counts):
    brick = (BX, BY, BZ)
    shape = jax.ShapeDtypeStruct
    anywhere = pl.BlockSpec(memory_space=pl.ANY)
    vmem = pltpu.VMEM
    dma = pltpu.SemaphoreType.DMA
    room = 58 * 1024 * 1024
    table_z, table_y, table_x, lam_xy, lam_z = tables()
    gas_shapes = (
        shape(brick, f32),
        shape((3,) + brick, f32),
        shape(brick, f32),
        shape((9,) + brick, f32),
    )
    *gas, waves = pl.pallas_call(
        kernel,
        out_shape=gas_shapes + (shape((3, NZ, 128), f32),),
        in_specs=[anywhere] * 9 + [pl.BlockSpec(memory_space=pltpu.SMEM)],
        out_specs=(anywhere,) * 5,
        scratch_shapes=[
            vmem((14, BX + 2, BY, BZ), f32),
            vmem((BX + 2, BY, BZ), f32),
            vmem(brick, f32),
            vmem(brick, jnp.int32),
            vmem((2, NZ, 2 * BZ), bf16),
            vmem((2, NY, NY), bf16),
            vmem((2, 2 * NX, NX), bf16),
            vmem((NX, NY), f32),
            vmem((14,) + brick, f32),
            vmem((2, NZ, 128), f32),
            vmem((16, 2, 16, 128), f32),
            vmem((2, 128, 128), f32),
            vmem((128, NY), f32),
            vmem((128, NY), f32),
            vmem((128, NY + 128), f32),
            vmem((128, NY + 128), f32),
            vmem((2, 2, 128, 128), f32),
            vmem((8, 3, 16, 128), f32),
            vmem((2, BX, 16, BZ), f32),
            vmem((2, BX, 16, BZ), f32),
            vmem((BX, 8, 128), f32),
            vmem((BX, 8, 128), f32),
            dma((9,)),
            dma((5,)),
            dma((4, 15)),
            dma((4, 15)),
            dma((9,)),
            dma((9,)),
        ],
        compiler_params=pltpu.CompilerParams(
            collective_id=0, has_side_effects=True, vmem_limit_bytes=room
        ),
        name="step",
    )(density, velocity, pressure, species, counts, table_z, table_y, table_x, lam_xy, lam_z)
    return pl.pallas_call(
        finish,
        out_shape=gas_shapes + (shape(brick, f32),),
        in_specs=[anywhere] * 8,
        out_specs=(anywhere,) * 5,
        scratch_shapes=[
            vmem(brick, f32),
            vmem((3,) + brick, f32),
            vmem(brick, f32),
            vmem((3,) + brick, f32),
            vmem(brick, f32),
            vmem((9,) + brick, f32),
            vmem((3, NZ, 128), f32),
            vmem((2, NZ, 2 * BZ), bf16),
            vmem((BX + 2, BY, BZ), f32),
            dma((8,)),
            dma((5,)),
        ],
        compiler_params=pltpu.CompilerParams(vmem_limit_bytes=room),
        name="finish",
    )(density, velocity, *gas, waves, table_z)


def solution(mesh):
    in_specs = (
        P("hx", "hy", "ga"),
        P(None, "hx", "hy", "ga"),
        P("hx", "hy", "ga"),
        P(None, "hx", "hy", "ga"),
        P("hx", "hy", "ga"),
    )
    out_specs = (
        P("hx", "hy", "ga"),
        P(None, "hx", "hy", "ga"),
        P("hx", "hy", "ga"),
        P(None, "hx", "hy", "ga"),
        P("hx", "hy", "ga"),
    )
    return jax.shard_map(local, mesh=mesh, in_specs=in_specs, out_specs=out_specs, check_vma=False)
```

```python
import functools

import jax
import jax.numpy as jnp
import ml_dtypes
import numpy as np
from jax import lax
from jax.experimental import pallas as pl
from jax.experimental.pallas import tpu as pltpu
from jax.sharding import PartitionSpec as P

NEWTON = 4
gamma_gas = 5.0 / 3.0
time_step = 0.1
half_step = 0.5 * time_step
cool_rates = (2.0, 5.0, 9.0, 14.0, 20.0, 3.0, 7.0, 11.0, 29.0)
NX, NY, NZ = 128, 256, 256
BX, BY, BZ = 8, 32, 128
MESH = pl.DeviceIdType.MESH
f32 = jnp.float32
bf16 = jnp.bfloat16


def cas_table(length):
    keys = np.arange(length)
    angle = 2.0 * np.pi / length * (keys[:, None] * keys[None, :] % length)
    return np.cos(angle) + np.sin(angle)


def halves(table):
    table = table.astype(np.float32)
    high = table.astype(ml_dtypes.bfloat16)
    low = (table - high.astype(np.float32)).astype(ml_dtypes.bfloat16)
    return np.stack([high, low])


def line_tables():
    blocks = NX // BX
    inner = BX - 1
    lam_y = 4.0 * np.sin(np.pi * np.arange(NY) / NY) ** 2
    lam_z = 4.0 * np.sin(np.pi * np.arange(NZ) / NZ) ** 2
    center = 2.0 + lam_z[:, None] + lam_y[None, :]
    factors = [1.0 / center]
    for _ in range(inner - 1):
        factors.append(1.0 / (center - factors[-1]))
    near = factors[-1]
    far = np.prod(np.stack(factors), axis=0)
    sweep = np.stack(factors + [center], axis=0).reshape(BX, blocks, NZ // blocks, NY)
    waves = np.arange(blocks)
    values = (center - 2.0 * near)[:, None, :] - 2.0 * far[:, None, :] * np.cos(
        2.0 * np.pi * waves / blocks
    )[None, :, None]
    values[0, 0, 0] = 1.0
    inverse = 1.0 / (blocks * values)
    bow = sum((x + 1) * (inner - x) for x in range(inner)) / 2.0
    inverse[0, 0, 0] = bow / (BX * BX * blocks)
    green = np.zeros((NZ, 48, NY // 2))
    green[:, 0:16] = inverse[:, :, 0 : NY // 2]
    green[:, 16:32] = inverse[:, :, NY // 2 :]
    green[0, 32:34, 0] = -1.0 / (BX * blocks)
    table = cas_table(blocks)
    mix = np.zeros((48, blocks, 8))
    spread = np.zeros((blocks, 8, 48))
    for part in range(2):
        rows = slice(16 * part, 16 * part + 16)
        mix[rows, :, 2 * part] = table
        mix[rows, :, 2 * part + 1] = np.roll(table, 1, axis=1)
        spread[:, 2 * part, rows] = np.roll(table, 1, axis=0)
        spread[:, 2 * part + 1, rows] = table
    mix[32, :, 4] = 1.0
    mix[33] = mix[0]
    spread[:, 0:2, 32] = 1.0
    spread[:, 4, 33] = 1.0
    return (
        halves(mix.reshape(48, 8 * blocks)),
        halves(spread.reshape(8 * blocks, 48)),
        green.astype(np.float32),
        np.moveaxis(sweep, 0, 1).astype(np.float32),
    )


def tables():
    table_y = cas_table(NY) / 256.0
    table_z = cas_table(NZ)
    parts = []
    for rank in range(NZ // BZ):
        first = rank * BZ
        edges = np.zeros((NZ, BZ))
        edges[:, 0] = table_z[:, (first - 1) % NZ]
        edges[:, BZ - 1] = table_z[:, (first + BZ) % NZ]
        parts.append(halves(np.concatenate([table_z[:, first : first + BZ], edges], axis=1)))
    return (np.stack(parts), halves(table_y)) + line_tables()


def split(values):
    high = values.astype(bf16)
    return high, (values - high.astype(f32)).astype(bf16)


def dot3(left, right, dims=(((1,), (0,)), ((), ()))):
    def one(i, j):
        return lax.dot_general(left[i], right[j], dims, preferred_element_type=f32)

    return one(0, 0) + (one(0, 1) + one(1, 0))


def swap_chunks(tiles, lane):
    low = lane < 64
    even = (lane // 32) % 2 == 0
    mid = [None] * 4
    for i in range(2):
        mid[i] = jnp.where(low, tiles[i], pltpu.roll(tiles[i + 2], 64, 1))
        mid[i + 2] = jnp.where(low, pltpu.roll(tiles[i], 64, 1), tiles[i + 2])
    out = [None] * 4
    for i in (0, 2):
        out[i] = jnp.where(even, mid[i], pltpu.roll(mid[i + 1], 32, 1))
        out[i + 1] = jnp.where(even, pltpu.roll(mid[i], 96, 1), mid[i + 1])
    return out


def kernel(
    density, velocity, pressure, species, counts, tz_in, ty_in, mix_in, spread_in, green_in, sweep_in,
    o_density, o_momentum, o_energy, o_species, b_buf,
    gas, sound, press, count, tz, ty, mix, spread, green, sweep, out,
    z_src, z_buf, u_buf, d_buf, y_src, x_buf, x_src, w_buf, b_src,
    yp_src, yp_buf, zp_src, zp_buf,
    in_sem, out_sem, send_sem, recv_sem, halo_send, halo_recv,
):
    a = lax.axis_index("hx")
    b = lax.axis_index("hy")
    g = lax.axis_index("ga")
    q = g * 8 + b
    side = lax.rem(g + a, 2)
    chunk = side * 8 + b

    loads = [
        (density, gas.at[0, pl.ds(1, BX)]),
        (tz_in.at[g], tz),
        (velocity, gas.at[pl.ds(1, 3), pl.ds(1, BX)]),
        (species, gas.at[pl.ds(5, 9), pl.ds(1, BX)]),
        (pressure, press),
        (counts, count),
        (ty_in, ty),
        (mix_in, mix),
        (spread_in, spread),
        (green_in.at[chunk * 16 + a], green),
        (sweep_in.at[chunk], sweep),
    ]
    loads = [pltpu.make_async_copy(s, d, in_sem.at[i]) for i, (s, d) in enumerate(loads)]
    for load in loads:
        load.start()

    barrier = pltpu.get_barrier_semaphore()

    def outward(n, middle):
        return middle + ((n + 1) // 2) * (2 * lax.rem(n, 2) - 1)

    def plane_id(n):
        t_b = lax.rem(b + outward(n // 2, 4), 8)
        t_g = lax.rem(g + 1 + n, 2)
        return t_b, t_g, {"hy": t_b, "ga": t_g}

    def line_id(n):
        t = lax.rem(a + outward(n, 8), 16)
        return t, {"hx": t, "ga": lax.rem(side + t, 2)}

    above = {"hx": lax.rem(a + 1, 16)}
    below = {"hx": lax.rem(a + 15, 16)}

    @pl.loop(0, 15)
    def _(n):
        pl.semaphore_signal(barrier, inc=1, device_id=plane_id(n)[2], device_id_type=MESH)
        pl.semaphore_signal(barrier, inc=1, device_id=line_id(n)[1], device_id_type=MESH)

    pl.semaphore_signal(barrier, inc=1, device_id=above, device_id_type=MESH)
    pl.semaphore_signal(barrier, inc=1, device_id=below, device_id_type=MESH)

    def remote(src, dst, sems, slot, target):
        return pltpu.make_async_remote_copy(
            src_ref=src, dst_ref=dst, send_sem=sems[0].at[slot], recv_sem=sems[1].at[slot],
            device_id=target, device_id_type=MESH,
        )

    rounds = [(send_sem.at[r], recv_sem.at[r]) for r in range(4)]

    def send1(n):
        t_b, t_g, where = plane_id(n)
        t = lax.rem(t_g + a, 2) * 8 + t_b
        return remote(z_src.at[:, pl.ds(t * 16, 16)], z_buf.at[q], rounds[0], n, where)

    def send2(n):
        t, where = line_id(n)
        return remote(y_src.at[pl.ds(t * 8, 8)], x_buf.at[pl.ds(a * 8, 8)], rounds[1], n, where)

    def send3(n):
        t, where = line_id(n)
        return remote(x_src.at[pl.ds(t * 8, 8)], w_buf.at[pl.ds(a * 8, 8)], rounds[2], n, where)

    def send4(n):
        t_b, _, where = plane_id(n)
        return remote(b_src.at[t_b], b_buf.at[:, pl.ds(chunk * 16, 16)], rounds[3], n, where)

    def start_all(send):
        @pl.loop(0, 15)
        def _(n):
            send(n).start()

    def arrive_all(send):
        @pl.loop(0, 15)
        def _(n):
            send(n).wait_recv()

    lane16 = lax.broadcasted_iota(jnp.int32, (16, 128), 1)

    loads[0].wait()
    loads[1].wait()
    brick = split(gas[0, pl.ds(1, BX)].reshape(BX * BY, BZ) - 1.0)
    turned = dot3((tz[0, :, 0:BZ], tz[1, :, 0:BZ]), brick, (((1,), (1,)), ((), ())))
    z_src[0] = turned[:, 0:128]
    z_src[1] = turned[:, 128:256]
    pl.semaphore_wait(barrier, 32)
    start_all(send1)
    z_buf[q] = z_src[:, pl.ds(pl.multiple_of(chunk * 16, 16), 16)]

    halos = (halo_send, halo_recv)
    right = {"hy": lax.rem(b + 1, 8)}
    left = {"hy": lax.rem(b + 7, 8)}
    other = {"ga": 1 - g}
    loads[2].wait()
    loads[3].wait()
    face_early = []
    for slot, (first, many) in enumerate(((0, 4), (5, 9))):
        rows = pl.ds(first, many)
        face_early.append(remote(gas.at[rows, BX], gas.at[rows, 0], halos, 2 * slot, above))
        face_early.append(remote(gas.at[rows, 1], gas.at[rows, BX + 1], halos, 2 * slot + 1, below))
    for face in face_early:
        face.start()
    loads[4].wait()
    loads[5].wait()
    lane8 = lax.broadcasted_iota(jnp.int32, (8, 128), 1)

    def cell_sound(p):
        return jnp.sqrt(gamma_gas * gas[4, p] / gas[0, p])

    @pl.loop(0, BX)
    def _(i):
        p = i + 1
        rho = gas[0, p]
        cooling = cool_rates[0] * gas[5, p]
        for s in range(1, 9):
            cooling = cooling + cool_rates[s] * gas[5 + s, p]
        stiffness = time_step * rho * cooling
        initial = press[i] / ((gamma_gas - 1.0) * rho)
        many = count[i]
        energy = initial
        for step in range(NEWTON):
            near = 1.0 + energy
            square = near * near
            top = (energy - initial) * square + stiffness * energy * energy * near
            bottom = square + stiffness * energy * (energy + 2.0)
            energy = jnp.where(many > step, energy - top / bottom, energy)
        gas[4, p] = (gamma_gas - 1.0) * rho * energy
        sound[p] = jnp.sqrt(gamma_gas * (gamma_gas - 1.0) * energy)
        tile = jnp.zeros((8, 128), f32)
        for f in range(15):
            field = gas[f, p] if f < 14 else sound[p]
            yp_src[0, i, f : f + 1, :] = field[BY - 1 : BY]
            yp_src[1, i, f : f + 1, :] = field[0:1]
            for j in range(4):
                moved = pltpu.roll(field[8 * j : 8 * j + 8], 32 * j + 2 * f + 1, 1)
                tile = jnp.where(lane8 // 2 == 16 * j + f, moved, tile)
        zp_src[i] = tile
        yp_src[0, i, 15:16, :] = jnp.zeros((1, 128), f32)
        yp_src[1, i, 15:16, :] = jnp.zeros((1, 128), f32)

    face_late = [
        remote(yp_src.at[0], yp_buf.at[0], halos, 6, right),
        remote(yp_src.at[1], yp_buf.at[1], halos, 7, left),
        remote(zp_src, zp_buf, halos, 8, other),
        remote(gas.at[4, BX], gas.at[4, 0], halos, 4, above),
        remote(gas.at[4, 1], gas.at[4, BX + 1], halos, 5, below),
    ]
    for face in face_late:
        face.start()

    row32 = lax.broadcasted_iota(jnp.int32, (BY, BZ), 0)
    lane32 = lax.broadcasted_iota(jnp.int32, (BY, BZ), 1)

    def hydro(i):
        p = i + 1

        def at(f, where):
            return gas[f, where] if f < 14 else sound[where]

        def sides(f, d):
            if d == 0:
                return at(f, p - 1), at(f, p + 1)
            field = at(f, p)
            if d == 1:
                lower = jnp.where(row32 == 0, yp_buf[0, i, f : f + 1, :], pltpu.roll(field, 1, 0))
                upper = jnp.where(
                    row32 == BY - 1, yp_buf[1, i, f : f + 1, :], pltpu.roll(field, BY - 1, 0)
                )
                return lower, upper
            tile = zp_buf[i]
            edge = jnp.concatenate(
                [pltpu.roll(tile, (BZ - 1 - 32 * j - 2 * f) % 128, 1) for j in range(4)], axis=0
            )
            lower = pltpu.roll(jnp.where(lane32 == BZ - 1, edge, field), 1, 1)
            upper = pltpu.roll(jnp.where(lane32 == 0, edge, field), BZ - 1, 1)
            return lower, upper

        rho = gas[0, p]
        vel = [gas[1 + k, p] for k in range(3)]
        cs = sound[p]
        keep = 1.0
        weights = []
        new_rho = 0.0
        new_energy = 0.0
        new_mom = [0.0, 0.0, 0.0]
        for d in range(3):
            rho_l, rho_u = sides(0, d)
            v_l, v_u = zip(*[sides(1 + k, d) for k in range(3)])
            p_l, p_u = sides(4, d)
            c_l, c_u = sides(14, d)
            here = jnp.abs(vel[d]) + cs
            w_l = jnp.maximum(here, jnp.abs(v_l[d]) + c_l)
            w_u = jnp.maximum(here, jnp.abs(v_u[d]) + c_u)
            b_l = half_step * (w_l + v_l[d])
            b_u = half_step * (w_u - v_u[d])
            a_l = b_l * rho_l
            a_u = b_u * rho_u
            keep = keep - half_step * (w_l + w_u)
            weights.append((a_l, a_u))
            new_rho = new_rho + (a_l + a_u)
            for k in range(3):
                new_mom[k] = new_mom[k] + (a_l * v_l[k] + a_u * v_u[k])
            new_mom[d] = new_mom[d] + half_step * (p_l - p_u)
            sq_l = v_l[0] * v_l[0] + v_l[1] * v_l[1] + v_l[2] * v_l[2]
            sq_u = v_u[0] * v_u[0] + v_u[1] * v_u[1] + v_u[2] * v_u[2]
            new_energy = new_energy + (
                0.5 * (a_l * sq_l + a_u * sq_u)
                + p_l * (1.5 * b_l + half_step * v_l[d])
                + p_u * (1.5 * b_u - half_step * v_u[d])
            )
        mass = keep * rho
        out[0, i] = new_rho + mass
        for k in range(3):
            out[1 + k, i] = new_mom[k] + mass * vel[k]
        sq = vel[0] * vel[0] + vel[1] * vel[1] + vel[2] * vel[2]
        out[4, i] = new_energy + keep * (1.5 * gas[4, p]) + 0.5 * mass * sq
        for s in range(5, 14):
            result = mass * gas[s, p]
            for d in range(3):
                lower, upper = sides(s, d)
                result = result + (weights[d][0] * lower + weights[d][1] * upper)
            out[s, i] = result

    loads[6].wait()
    arrive_all(send1)
    for hi in range(2):
        for xh in range(2):
            tiles = [z_buf[4 * hi + i, xh] + z_buf[8 + 4 * hi + i, xh] for i in range(4)]
            tiles = swap_chunks(tiles, lane16)
            for xl in range(4):
                x = 4 * xh + xl
                u_buf[16 * x : 16 * x + 16, 128 * hi : 128 * hi + 128] = tiles[xl]
    table_y = (ty[0], ty[1])
    d_buf[...] = dot3(split(u_buf[...]), table_y)

    for load in loads[7:]:
        load.wait()

    def plane(x):
        return d_buf[16 * x : 16 * x + 16, :]

    def inside(before, after, mean):
        values = []
        carry = before
        for x in range(BX - 1):
            carry = carry + (mean - plane(x))
            if x == BX - 2:
                carry = carry + after
            carry = carry * sweep[x]
            values.append(carry)
        for x in range(BX - 3, -1, -1):
            values[x] = values[x] + sweep[x] * values[x + 1]
        return values

    values = inside(0.0, 0.0, 0.0)
    last = values[BX - 2] - plane(BX - 1)
    first = values[0]
    whole = functools.reduce(lambda p, r: p + r, [v[:, 0:128] for v in values])
    y_src[...] = jnp.zeros((128, 128), f32)
    for r, row in enumerate((last[:, 0:128], first[:, 0:128], last[:, 128:], first[:, 128:], whole)):
        y_src[pl.ds(r, 16, stride=8), :] = row
    start_all(send2)
    x_buf[pl.ds(pl.multiple_of(a * 8, 8), 8)] = y_src[pl.ds(pl.multiple_of(a * 8, 8), 8)]

    for face in face_late[0:3]:
        face.wait_recv()

    @pl.loop(1, 4)
    def _(i):
        hydro(i)

    arrive_all(send2)
    waves = dot3((mix[0], mix[1]), split(x_buf[...])) * green[...]
    x_src[...] = dot3((spread[0], spread[1]), split(waves))
    start_all(send3)
    w_buf[pl.ds(pl.multiple_of(a * 8, 8), 8)] = x_src[pl.ds(pl.multiple_of(a * 8, 8), 8)]

    @pl.loop(4, 7)
    def _(i):
        hydro(i)

    arrive_all(send3)

    def returned(r):
        return w_buf[pl.ds(r, 16, stride=8), :]

    before = jnp.concatenate([returned(0), returned(2)], axis=1)
    own_plane = jnp.concatenate([returned(1), returned(3)], axis=1)
    mean = returned(4)
    mean = jnp.concatenate([mean, jnp.zeros_like(mean)], axis=1)
    values = inside(before, own_plane, mean)
    beyond = sweep[BX - 1] * own_plane - values[BX - 2] + (plane(BX - 1) - mean)
    back = dot3(split(jnp.concatenate(values + [own_plane, before, beyond], axis=0)), table_y)

    def line(hi, row):
        return back[16 * row : 16 * row + 16, 128 * hi : 128 * hi + 128]

    spot = lane16 % 32
    for hi in range(2):
        rows_low = jnp.zeros((16, 128), f32)
        rows_high = rows_low
        for xh in range(2):
            tiles = [line(hi, 4 * xh + xl) for xl in range(4)]
            outer = [line(1 - hi, 4 * xh + xl) for xl in range(4)]
            for xl in range(4):
                x = 4 * xh + xl
                low = jnp.where(
                    lane16 < 32, pltpu.roll(outer[xl], 1 + x, 1), pltpu.roll(tiles[xl], 1 + x, 1)
                )
                high = jnp.where(
                    lane16 >= 96, pltpu.roll(outer[xl], 96 + x, 1), pltpu.roll(tiles[xl], 96 + x, 1)
                )
                rows_low = jnp.where(spot == x, low, rows_low)
                rows_high = jnp.where(spot == x, high, rows_high)
            tiles = swap_chunks(tiles, lane16)
            for i in range(4):
                b_src[4 * hi + i, xh] = tiles[i]
        tiles = swap_chunks([line(hi, 8), line(hi, 9), rows_low, rows_high], lane16)
        for i in range(4):
            b_src[4 * hi + i, 2] = tiles[i]
    start_all(send4)
    own = pltpu.make_async_copy(b_src.at[b], b_buf.at[:, pl.ds(chunk * 16, 16)], out_sem.at[4])
    own.start()

    for face in face_early + face_late[3:5]:
        face.wait_recv()
    sound[0] = cell_sound(0)
    sound[BX + 1] = cell_sound(BX + 1)

    @pl.loop(0, 2)
    def _(i):
        hydro(i * (BX - 1))

    stores = [
        own,
        pltpu.make_async_copy(out.at[0], o_density, out_sem.at[0]),
        pltpu.make_async_copy(out.at[pl.ds(1, 3)], o_momentum, out_sem.at[1]),
        pltpu.make_async_copy(out.at[4], o_energy, out_sem.at[2]),
        pltpu.make_async_copy(out.at[pl.ds(5, 9)], o_species, out_sem.at[3]),
    ]
    for store in stores[1:]:
        store.start()

    for send in (send1, send2, send3, send4):

        @pl.loop(0, 15)
        def _(n):
            send(n).wait_send()

    for face in face_early + face_late:
        face.wait_send()
    for store in stores:
        store.wait()
    arrive_all(send4)


def finish(
    density, velocity, density_in, momentum_in, energy_in, species_in, waves, tz_in,
    o_density, o_momentum, o_energy, o_species, o_potential,
    rho, vel, new_rho, mom, energy, frac, spec, tz, pot, load_sem, store_sem,
):
    loads = [
        (waves, spec),
        (tz_in.at[lax.axis_index("ga")], tz),
        (density_in, new_rho),
        (species_in, frac),
        (density, rho),
        (velocity, vel),
        (momentum_in, mom),
        (energy_in, energy),
    ]
    loads = [pltpu.make_async_copy(s, d, load_sem.at[i]) for i, (s, d) in enumerate(loads)]
    stores = [
        (new_rho, o_density),
        (frac, o_species),
        (pot.at[pl.ds(1, BX)], o_potential),
        (mom, o_momentum),
        (energy, o_energy),
    ]
    stores = [pltpu.make_async_copy(s, d, store_sem.at[i]) for i, (s, d) in enumerate(stores)]
    for load in loads:
        load.start()
    loads[0].wait()
    loads[1].wait()
    table = (tz[0], tz[1])
    edges = []
    for xh in range(2):
        done = dot3(split(spec[xh].T), table)
        edges.append(done[:, BZ:])
        for xl in range(4):
            pot[1 + 4 * xh + xl] = done[32 * xl : 32 * xl + 32, 0:BZ]
    stores[2].start()
    done = dot3(split(spec[2].T), (tz[0, :, 0:BZ], tz[1, :, 0:BZ]))
    pot[0] = done[0:32]
    pot[BX + 1] = done[32:64]
    for i in range(2):
        loads[2 + i].wait()
        stores[i].start()
    for load in loads[4:]:
        load.wait()
    row32 = lax.broadcasted_iota(jnp.int32, (BY, BZ), 0)
    lane32 = lax.broadcasted_iota(jnp.int32, (BY, BZ), 1)
    for i in range(BX):
        here = pot[1 + i]
        edge = edges[i // 4][32 * (i % 4) : 32 * (i % 4) + 32]
        pull = [
            pot[i] - pot[i + 2],
            jnp.where(row32 == 0, done[64 + i : 65 + i], pltpu.roll(here, 1, 0))
            - jnp.where(row32 == BY - 1, done[96 + i : 97 + i], pltpu.roll(here, BY - 1, 0)),
            jnp.where(lane32 == 0, edge, pltpu.roll(here, 1, 1))
            - jnp.where(lane32 == BZ - 1, edge, pltpu.roll(here, BZ - 1, 1)),
        ]
        weight = half_step * rho[i]
        work = energy[i]
        for k in range(3):
            push = weight * pull[k]
            mom[k, i] = mom[k, i] + push
            work = work + push * vel[k, i]
        energy[i] = work
    stores[3].start()
    stores[4].start()
    for store in stores:
        store.wait()


def local(density, velocity, pressure, species, counts):
    brick = (BX, BY, BZ)
    shape = jax.ShapeDtypeStruct
    anywhere = pl.BlockSpec(memory_space=pl.ANY)
    vmem = pltpu.VMEM
    dma = pltpu.SemaphoreType.DMA
    room = 58 * 1024 * 1024
    table_z, *others = tables()
    gas_shapes = (
        shape(brick, f32),
        shape((3,) + brick, f32),
        shape(brick, f32),
        shape((9,) + brick, f32),
    )
    *gas, waves = pl.pallas_call(
        kernel,
        out_shape=gas_shapes + (shape((3, NZ, 128), f32),),
        in_specs=[anywhere] * 11,
        out_specs=(anywhere,) * 5,
        scratch_shapes=[
            vmem((14, BX + 2, BY, BZ), f32),
            vmem((BX + 2, BY, BZ), f32),
            vmem(brick, f32),
            vmem(brick, jnp.int32),
            vmem((2, NZ, 2 * BZ), bf16),
            vmem((2, NY, NY), bf16),
            vmem((2, 48, 128), bf16),
            vmem((2, 128, 48), bf16),
            vmem((48, NY // 2), f32),
            vmem((BX, 16, NY), f32),
            vmem((14,) + brick, f32),
            vmem((2, NZ, 128), f32),
            vmem((16, 2, 16, 128), f32),
            vmem((128, NY), f32),
            vmem((128, NY), f32),
            vmem((128, 128), f32),
            vmem((128, 128), f32),
            vmem((128, 128), f32),
            vmem((128, 128), f32),
            vmem((8, 3, 16, 128), f32),
            vmem((2, BX, 16, BZ), f32),
            vmem((2, BX, 16, BZ), f32),
            vmem((BX, 8, 128), f32),
            vmem((BX, 8, 128), f32),
            dma((11,)),
            dma((5,)),
            dma((4, 15)),
            dma((4, 15)),
            dma((9,)),
            dma((9,)),
        ],
        compiler_params=pltpu.CompilerParams(
            collective_id=0, has_side_effects=True, vmem_limit_bytes=room
        ),
        name="step",
    )(density, velocity, pressure, species, counts, table_z, *others)
    return pl.pallas_call(
        finish,
        out_shape=gas_shapes + (shape(brick, f32),),
        in_specs=[anywhere] * 8,
        out_specs=(anywhere,) * 5,
        scratch_shapes=[
            vmem(brick, f32),
            vmem((3,) + brick, f32),
            vmem(brick, f32),
            vmem((3,) + brick, f32),
            vmem(brick, f32),
            vmem((9,) + brick, f32),
            vmem((3, NZ, 128), f32),
            vmem((2, NZ, 2 * BZ), bf16),
            vmem((BX + 2, BY, BZ), f32),
            dma((8,)),
            dma((5,)),
        ],
        compiler_params=pltpu.CompilerParams(vmem_limit_bytes=room),
        name="finish",
    )(density, velocity, *gas, waves, table_z)


def solution(mesh):
    in_specs = (
        P("hx", "hy", "ga"),
        P(None, "hx", "hy", "ga"),
        P("hx", "hy", "ga"),
        P(None, "hx", "hy", "ga"),
        P("hx", "hy", "ga"),
    )
    out_specs = (
        P("hx", "hy", "ga"),
        P(None, "hx", "hy", "ga"),
        P("hx", "hy", "ga"),
        P(None, "hx", "hy", "ga"),
        P("hx", "hy", "ga"),
    )
    return jax.shard_map(local, mesh=mesh, in_specs=in_specs, out_specs=out_specs, check_vma=False)
```

```python
import functools

import jax
import jax.numpy as jnp
import ml_dtypes
import numpy as np
from jax import lax
from jax.experimental import pallas as pl
from jax.experimental.pallas import tpu as pltpu
from jax.sharding import PartitionSpec as P

NEWTON = 4
gamma_gas = 5.0 / 3.0
time_step = 0.1
half_step = 0.5 * time_step
cool_rates = (2.0, 5.0, 9.0, 14.0, 20.0, 3.0, 7.0, 11.0, 29.0)
NX, NY, NZ = 128, 256, 256
BX, BY, BZ = 8, 32, 128
MESH = pl.DeviceIdType.MESH
f32 = jnp.float32
bf16 = jnp.bfloat16


def cas_table(length):
    keys = np.arange(length)
    angle = 2.0 * np.pi / length * (keys[:, None] * keys[None, :] % length)
    return np.cos(angle) + np.sin(angle)


def halves(table):
    table = table.astype(np.float32)
    high = table.astype(ml_dtypes.bfloat16)
    low = (table - high.astype(np.float32)).astype(ml_dtypes.bfloat16)
    return np.stack([high, low])


def line_tables():
    blocks = NX // BX
    inner = BX - 1
    lam_y = 4.0 * np.sin(np.pi * np.arange(NY) / NY) ** 2
    lam_z = 4.0 * np.sin(np.pi * np.arange(NZ) / NZ) ** 2
    center = 2.0 + lam_z[:, None] + lam_y[None, :]
    factors = [1.0 / center]
    for _ in range(inner - 1):
        factors.append(1.0 / (center - factors[-1]))
    near = factors[-1]
    far = np.prod(np.stack(factors), axis=0)
    sweep = np.stack(factors + [center], axis=0).reshape(BX, blocks, NZ // blocks, NY)
    waves = np.arange(blocks)
    values = (center - 2.0 * near)[:, None, :] - 2.0 * far[:, None, :] * np.cos(
        2.0 * np.pi * waves / blocks
    )[None, :, None]
    values[0, 0, 0] = 1.0
    inverse = 1.0 / (blocks * values)
    bow = sum((x + 1) * (inner - x) for x in range(inner)) / 2.0
    inverse[0, 0, 0] = bow / (BX * BX * blocks)
    green = np.zeros((NZ, 48, NY // 2))
    green[:, 0:16] = inverse[:, :, 0 : NY // 2]
    green[:, 16:32] = inverse[:, :, NY // 2 :]
    green[0, 32:34, 0] = -1.0 / (BX * blocks)
    table = cas_table(blocks)
    mix = np.zeros((48, blocks, 8))
    spread = np.zeros((blocks, 8, 48))
    for part in range(2):
        rows = slice(16 * part, 16 * part + 16)
        mix[rows, :, 2 * part] = table
        mix[rows, :, 2 * part + 1] = np.roll(table, 1, axis=1)
        spread[:, 2 * part, rows] = np.roll(table, 1, axis=0)
        spread[:, 2 * part + 1, rows] = table
    mix[32, :, 4] = 1.0
    mix[33] = mix[0]
    spread[:, 0:2, 32] = 1.0
    spread[:, 4, 33] = 1.0
    return (
        halves(mix.reshape(48, 8 * blocks)),
        halves(spread.reshape(8 * blocks, 48)),
        green.astype(np.float32),
        np.moveaxis(sweep, 0, 1).astype(np.float32),
    )


def tables():
    table_y = cas_table(NY) / 256.0
    table_z = cas_table(NZ)
    parts = []
    for rank in range(NZ // BZ):
        first = rank * BZ
        edges = np.zeros((NZ, BZ))
        edges[:, 0] = table_z[:, (first - 1) % NZ]
        edges[:, BZ - 1] = table_z[:, (first + BZ) % NZ]
        parts.append(halves(np.concatenate([table_z[:, first : first + BZ], edges], axis=1)))
    return (np.stack(parts), halves(table_y)) + line_tables()


def split(values):
    high = values.astype(bf16)
    return high, (values - high.astype(f32)).astype(bf16)


def dot3(left, right, dims=(((1,), (0,)), ((), ()))):
    def one(i, j):
        return lax.dot_general(left[i], right[j], dims, preferred_element_type=f32)

    return one(0, 0) + (one(0, 1) + one(1, 0))


def swap_chunks(tiles, lane):
    low = lane < 64
    even = (lane // 32) % 2 == 0
    mid = [None] * 4
    for i in range(2):
        mid[i] = jnp.where(low, tiles[i], pltpu.roll(tiles[i + 2], 64, 1))
        mid[i + 2] = jnp.where(low, pltpu.roll(tiles[i], 64, 1), tiles[i + 2])
    out = [None] * 4
    for i in (0, 2):
        out[i] = jnp.where(even, mid[i], pltpu.roll(mid[i + 1], 32, 1))
        out[i + 1] = jnp.where(even, pltpu.roll(mid[i], 96, 1), mid[i + 1])
    return out


def kernel(
    density, velocity, pressure, species, counts, tz_in, ty_in, mix_in, spread_in, green_in, sweep_in,
    o_density, o_momentum, o_energy, o_species, b_buf,
    gas, sound, press, count, tz, ty, mix, spread, green, sweep, out,
    z_src, z_buf, u_buf, d_buf, y_src, x_buf, x_src, w_buf, b_src,
    yp_src, yp_buf, zp_src, zp_buf,
    in_sem, out_sem, send_sem, recv_sem, halo_send, halo_recv,
):
    a = lax.axis_index("hx")
    b = lax.axis_index("hy")
    g = lax.axis_index("ga")
    q = g * 8 + b
    side = lax.rem(g + a, 2)
    chunk = side * 8 + b

    loads = [
        (density, gas.at[0, pl.ds(1, BX)]),
        (tz_in.at[g], tz),
        (velocity, gas.at[pl.ds(1, 3), pl.ds(1, BX)]),
        (species, gas.at[pl.ds(5, 9), pl.ds(1, BX)]),
        (pressure, press),
        (counts, count),
        (ty_in, ty),
        (mix_in, mix),
        (spread_in, spread),
        (green_in.at[chunk * 16 + a], green),
        (sweep_in.at[chunk], sweep),
    ]
    loads = [pltpu.make_async_copy(s, d, in_sem.at[i]) for i, (s, d) in enumerate(loads)]
    for load in loads:
        load.start()

    barrier = pltpu.get_barrier_semaphore()

    def outward(n, middle):
        return middle + ((n + 1) // 2) * (2 * lax.rem(n, 2) - 1)

    def plane_id(n):
        t_b = lax.rem(b + outward(n // 2, 4), 8)
        t_g = lax.rem(g + 1 + n, 2)
        return t_b, t_g, {"hy": t_b, "ga": t_g}

    def line_id(n):
        t = lax.rem(a + outward(n, 8), 16)
        return t, {"hx": t, "ga": lax.rem(side + t, 2)}

    above = {"hx": lax.rem(a + 1, 16)}
    below = {"hx": lax.rem(a + 15, 16)}

    @pl.loop(0, 15)
    def _(n):
        pl.semaphore_signal(barrier, inc=1, device_id=plane_id(n)[2], device_id_type=MESH)
        pl.semaphore_signal(barrier, inc=1, device_id=line_id(n)[1], device_id_type=MESH)

    pl.semaphore_signal(barrier, inc=1, device_id=above, device_id_type=MESH)
    pl.semaphore_signal(barrier, inc=1, device_id=below, device_id_type=MESH)

    def remote(src, dst, sems, slot, target):
        return pltpu.make_async_remote_copy(
            src_ref=src, dst_ref=dst, send_sem=sems[0].at[slot], recv_sem=sems[1].at[slot],
            device_id=target, device_id_type=MESH,
        )

    rounds = [(send_sem.at[r], recv_sem.at[r]) for r in range(4)]

    def send1(n):
        t_b, t_g, where = plane_id(n)
        t = lax.rem(t_g + a, 2) * 8 + t_b
        return remote(z_src.at[:, pl.ds(t * 16, 16)], z_buf.at[q], rounds[0], n, where)

    def send2(n):
        t, where = line_id(n)
        return remote(y_src.at[pl.ds(t * 8, 8)], x_buf.at[pl.ds(a * 8, 8)], rounds[1], n, where)

    def send3(n):
        t, where = line_id(n)
        return remote(x_src.at[pl.ds(t * 8, 8)], w_buf.at[pl.ds(a * 8, 8)], rounds[2], n, where)

    def send4(n):
        t_b, _, where = plane_id(n)
        return remote(b_src.at[t_b], b_buf.at[:, pl.ds(chunk * 16, 16)], rounds[3], n, where)

    def start_all(send):
        @pl.loop(0, 15)
        def _(n):
            send(n).start()

    def arrive_all(send):
        @pl.loop(0, 15)
        def _(n):
            send(n).wait_recv()

    lane16 = lax.broadcasted_iota(jnp.int32, (16, 128), 1)

    loads[0].wait()
    loads[1].wait()
    brick = split(gas[0, pl.ds(1, BX)].reshape(BX * BY, BZ) - 1.0)
    turned = dot3((tz[0, :, 0:BZ], tz[1, :, 0:BZ]), brick, (((1,), (1,)), ((), ())))
    z_src[0] = turned[:, 0:128]
    z_src[1] = turned[:, 128:256]
    pl.semaphore_wait(barrier, 32)
    start_all(send1)
    z_buf[q] = z_src[:, pl.ds(pl.multiple_of(chunk * 16, 16), 16)]

    halos = (halo_send, halo_recv)
    right = {"hy": lax.rem(b + 1, 8)}
    left = {"hy": lax.rem(b + 7, 8)}
    other = {"ga": 1 - g}
    loads[2].wait()
    loads[3].wait()
    face_early = []
    for slot, (first, many) in enumerate(((0, 4), (4, 5), (9, 5))):
        rows = pl.ds(first, many)
        face_early.append(remote(gas.at[rows, BX], gas.at[rows, 0], halos, 9 + 2 * slot, above))
        face_early.append(remote(gas.at[rows, 1], gas.at[rows, BX + 1], halos, 10 + 2 * slot, below))
    for face in face_early[0:2]:
        face.start()
    loads[4].wait()
    loads[5].wait()
    lane8 = lax.broadcasted_iota(jnp.int32, (8, 128), 1)

    def cell_sound(p):
        return jnp.sqrt(gamma_gas * gas[4, p] / gas[0, p])

    @pl.loop(0, BX)
    def _(i):
        p = i + 1
        rho = gas[0, p]
        cooling = cool_rates[0] * gas[5, p]
        for s in range(1, 9):
            cooling = cooling + cool_rates[s] * gas[5 + s, p]
        stiffness = time_step * rho * cooling
        initial = press[i] / ((gamma_gas - 1.0) * rho)
        many = count[i]
        energy = initial
        for step in range(NEWTON):
            near = 1.0 + energy
            square = near * near
            top = (energy - initial) * square + stiffness * energy * energy * near
            bottom = square + stiffness * energy * (energy + 2.0)
            energy = jnp.where(many > step, energy - top / bottom, energy)
        gas[4, p] = (gamma_gas - 1.0) * rho * energy
        sound[p] = jnp.sqrt(gamma_gas * (gamma_gas - 1.0) * energy)
        tile = jnp.zeros((8, 128), f32)
        for f in range(15):
            field = gas[f, p] if f < 14 else sound[p]
            yp_src[0, i, f : f + 1, :] = field[BY - 1 : BY]
            yp_src[1, i, f : f + 1, :] = field[0:1]
            for j in range(4):
                moved = pltpu.roll(field[8 * j : 8 * j + 8], 32 * j + 2 * f + 1, 1)
                tile = jnp.where(lane8 // 2 == 16 * j + f, moved, tile)
        zp_src[i] = tile
        yp_src[0, i, 15:16, :] = jnp.zeros((1, 128), f32)
        yp_src[1, i, 15:16, :] = jnp.zeros((1, 128), f32)

    face_late = [
        remote(yp_src.at[0], yp_buf.at[0], halos, 6, right),
        remote(yp_src.at[1], yp_buf.at[1], halos, 7, left),
        remote(zp_src, zp_buf, halos, 8, other),
    ]
    for face in face_late:
        face.start()

    row32 = lax.broadcasted_iota(jnp.int32, (BY, BZ), 0)
    lane32 = lax.broadcasted_iota(jnp.int32, (BY, BZ), 1)

    def hydro(i):
        p = i + 1

        def at(f, where):
            return gas[f, where] if f < 14 else sound[where]

        def sides(f, d):
            if d == 0:
                return at(f, p - 1), at(f, p + 1)
            field = at(f, p)
            if d == 1:
                lower = jnp.where(row32 == 0, yp_buf[0, i, f : f + 1, :], pltpu.roll(field, 1, 0))
                upper = jnp.where(
                    row32 == BY - 1, yp_buf[1, i, f : f + 1, :], pltpu.roll(field, BY - 1, 0)
                )
                return lower, upper
            tile = zp_buf[i]
            edge = jnp.concatenate(
                [pltpu.roll(tile, (BZ - 1 - 32 * j - 2 * f) % 128, 1) for j in range(4)], axis=0
            )
            lower = pltpu.roll(jnp.where(lane32 == BZ - 1, edge, field), 1, 1)
            upper = pltpu.roll(jnp.where(lane32 == 0, edge, field), BZ - 1, 1)
            return lower, upper

        rho = gas[0, p]
        vel = [gas[1 + k, p] for k in range(3)]
        cs = sound[p]
        keep = 1.0
        weights = []
        new_rho = 0.0
        new_energy = 0.0
        new_mom = [0.0, 0.0, 0.0]
        for d in range(3):
            rho_l, rho_u = sides(0, d)
            v_l, v_u = zip(*[sides(1 + k, d) for k in range(3)])
            p_l, p_u = sides(4, d)
            c_l, c_u = sides(14, d)
            here = jnp.abs(vel[d]) + cs
            w_l = jnp.maximum(here, jnp.abs(v_l[d]) + c_l)
            w_u = jnp.maximum(here, jnp.abs(v_u[d]) + c_u)
            b_l = half_step * (w_l + v_l[d])
            b_u = half_step * (w_u - v_u[d])
            a_l = b_l * rho_l
            a_u = b_u * rho_u
            keep = keep - half_step * (w_l + w_u)
            weights.append((a_l, a_u))
            new_rho = new_rho + (a_l + a_u)
            for k in range(3):
                new_mom[k] = new_mom[k] + (a_l * v_l[k] + a_u * v_u[k])
            new_mom[d] = new_mom[d] + half_step * (p_l - p_u)
            sq_l = v_l[0] * v_l[0] + v_l[1] * v_l[1] + v_l[2] * v_l[2]
            sq_u = v_u[0] * v_u[0] + v_u[1] * v_u[1] + v_u[2] * v_u[2]
            new_energy = new_energy + (
                0.5 * (a_l * sq_l + a_u * sq_u)
                + p_l * (1.5 * b_l + half_step * v_l[d])
                + p_u * (1.5 * b_u - half_step * v_u[d])
            )
        mass = keep * rho
        out[0, i] = new_rho + mass
        for k in range(3):
            out[1 + k, i] = new_mom[k] + mass * vel[k]
        sq = vel[0] * vel[0] + vel[1] * vel[1] + vel[2] * vel[2]
        out[4, i] = new_energy + keep * (1.5 * gas[4, p]) + 0.5 * mass * sq
        for s in range(5, 14):
            result = mass * gas[s, p]
            for d in range(3):
                lower, upper = sides(s, d)
                result = result + (weights[d][0] * lower + weights[d][1] * upper)
            out[s, i] = result

    loads[6].wait()
    arrive_all(send1)
    for hi in range(2):
        for xh in range(2):
            tiles = [z_buf[4 * hi + i, xh] + z_buf[8 + 4 * hi + i, xh] for i in range(4)]
            tiles = swap_chunks(tiles, lane16)
            for xl in range(4):
                x = 4 * xh + xl
                u_buf[16 * x : 16 * x + 16, 128 * hi : 128 * hi + 128] = tiles[xl]
    table_y = (ty[0], ty[1])
    d_buf[...] = dot3(split(u_buf[...]), table_y)

    for load in loads[7:]:
        load.wait()

    def plane(x):
        return d_buf[16 * x : 16 * x + 16, :]

    def inside(before, after, mean):
        values = []
        carry = before
        for x in range(BX - 1):
            carry = carry + (mean - plane(x))
            if x == BX - 2:
                carry = carry + after
            carry = carry * sweep[x]
            values.append(carry)
        for x in range(BX - 3, -1, -1):
            values[x] = values[x] + sweep[x] * values[x + 1]
        return values

    values = inside(0.0, 0.0, 0.0)
    last = values[BX - 2] - plane(BX - 1)
    first = values[0]
    whole = functools.reduce(lambda p, r: p + r, [v[:, 0:128] for v in values])
    y_src[...] = jnp.zeros((128, 128), f32)
    for r, row in enumerate((last[:, 0:128], first[:, 0:128], last[:, 128:], first[:, 128:], whole)):
        y_src[pl.ds(r, 16, stride=8), :] = row
    start_all(send2)
    for face in face_early[2:4]:
        face.start()
    x_buf[pl.ds(pl.multiple_of(a * 8, 8), 8)] = y_src[pl.ds(pl.multiple_of(a * 8, 8), 8)]

    for face in face_late[0:3]:
        face.wait_recv()

    @pl.loop(1, 4)
    def _(i):
        hydro(i)

    arrive_all(send2)
    waves = dot3((mix[0], mix[1]), split(x_buf[...])) * green[...]
    x_src[...] = dot3((spread[0], spread[1]), split(waves))
    start_all(send3)
    for face in face_early[4:6]:
        face.start()
    w_buf[pl.ds(pl.multiple_of(a * 8, 8), 8)] = x_src[pl.ds(pl.multiple_of(a * 8, 8), 8)]

    @pl.loop(4, 7)
    def _(i):
        hydro(i)

    arrive_all(send3)

    def returned(r):
        return w_buf[pl.ds(r, 16, stride=8), :]

    before = jnp.concatenate([returned(0), returned(2)], axis=1)
    own_plane = jnp.concatenate([returned(1), returned(3)], axis=1)
    mean = returned(4)
    mean = jnp.concatenate([mean, jnp.zeros_like(mean)], axis=1)
    values = inside(before, own_plane, mean)
    beyond = sweep[BX - 1] * own_plane - values[BX - 2] + (plane(BX - 1) - mean)
    back = dot3(split(jnp.concatenate(values + [own_plane, before, beyond], axis=0)), table_y)

    def line(hi, row):
        return back[16 * row : 16 * row + 16, 128 * hi : 128 * hi + 128]

    spot = lane16 % 32
    for hi in range(2):
        rows_low = jnp.zeros((16, 128), f32)
        rows_high = rows_low
        for xh in range(2):
            tiles = [line(hi, 4 * xh + xl) for xl in range(4)]
            outer = [line(1 - hi, 4 * xh + xl) for xl in range(4)]
            for xl in range(4):
                x = 4 * xh + xl
                low = jnp.where(
                    lane16 < 32, pltpu.roll(outer[xl], 1 + x, 1), pltpu.roll(tiles[xl], 1 + x, 1)
                )
                high = jnp.where(
                    lane16 >= 96, pltpu.roll(outer[xl], 96 + x, 1), pltpu.roll(tiles[xl], 96 + x, 1)
                )
                rows_low = jnp.where(spot == x, low, rows_low)
                rows_high = jnp.where(spot == x, high, rows_high)
            tiles = swap_chunks(tiles, lane16)
            for i in range(4):
                b_src[4 * hi + i, xh] = tiles[i]
        tiles = swap_chunks([line(hi, 8), line(hi, 9), rows_low, rows_high], lane16)
        for i in range(4):
            b_src[4 * hi + i, 2] = tiles[i]
    start_all(send4)
    own = pltpu.make_async_copy(b_src.at[b], b_buf.at[:, pl.ds(chunk * 16, 16)], out_sem.at[4])
    own.start()

    for face in face_early:
        face.wait_recv()
    sound[0] = cell_sound(0)
    sound[BX + 1] = cell_sound(BX + 1)

    @pl.loop(0, 2)
    def _(i):
        hydro(i * (BX - 1))

    stores = [
        own,
        pltpu.make_async_copy(out.at[0], o_density, out_sem.at[0]),
        pltpu.make_async_copy(out.at[pl.ds(1, 3)], o_momentum, out_sem.at[1]),
        pltpu.make_async_copy(out.at[4], o_energy, out_sem.at[2]),
        pltpu.make_async_copy(out.at[pl.ds(5, 9)], o_species, out_sem.at[3]),
    ]
    for store in stores[1:]:
        store.start()

    for send in (send1, send2, send3, send4):

        @pl.loop(0, 15)
        def _(n):
            send(n).wait_send()

    for face in face_early + face_late:
        face.wait_send()
    for store in stores:
        store.wait()
    arrive_all(send4)


def finish(
    density, velocity, density_in, momentum_in, energy_in, species_in, waves, tz_in,
    o_density, o_momentum, o_energy, o_species, o_potential,
    rho, vel, new_rho, mom, energy, frac, spec, tz, pot, load_sem, store_sem,
):
    loads = [
        (waves, spec),
        (tz_in.at[lax.axis_index("ga")], tz),
        (density_in, new_rho),
        (species_in, frac),
        (density, rho),
        (velocity, vel),
        (momentum_in, mom),
        (energy_in, energy),
    ]
    loads = [pltpu.make_async_copy(s, d, load_sem.at[i]) for i, (s, d) in enumerate(loads)]
    stores = [
        (new_rho, o_density),
        (frac, o_species),
        (pot.at[pl.ds(1, BX)], o_potential),
        (mom, o_momentum),
        (energy, o_energy),
    ]
    stores = [pltpu.make_async_copy(s, d, store_sem.at[i]) for i, (s, d) in enumerate(stores)]
    for load in loads:
        load.start()
    loads[0].wait()
    loads[1].wait()
    table = (tz[0], tz[1])
    edges = []
    for xh in range(2):
        done = dot3(split(spec[xh].T), table)
        edges.append(done[:, BZ:])
        for xl in range(4):
            pot[1 + 4 * xh + xl] = done[32 * xl : 32 * xl + 32, 0:BZ]
    stores[2].start()
    done = dot3(split(spec[2].T), (tz[0, :, 0:BZ], tz[1, :, 0:BZ]))
    pot[0] = done[0:32]
    pot[BX + 1] = done[32:64]
    for i in range(2):
        loads[2 + i].wait()
        stores[i].start()
    for load in loads[4:]:
        load.wait()
    row32 = lax.broadcasted_iota(jnp.int32, (BY, BZ), 0)
    lane32 = lax.broadcasted_iota(jnp.int32, (BY, BZ), 1)
    for i in range(BX):
        here = pot[1 + i]
        edge = edges[i // 4][32 * (i % 4) : 32 * (i % 4) + 32]
        pull = [
            pot[i] - pot[i + 2],
            jnp.where(row32 == 0, done[64 + i : 65 + i], pltpu.roll(here, 1, 0))
            - jnp.where(row32 == BY - 1, done[96 + i : 97 + i], pltpu.roll(here, BY - 1, 0)),
            jnp.where(lane32 == 0, edge, pltpu.roll(here, 1, 1))
            - jnp.where(lane32 == BZ - 1, edge, pltpu.roll(here, BZ - 1, 1)),
        ]
        weight = half_step * rho[i]
        work = energy[i]
        for k in range(3):
            push = weight * pull[k]
            mom[k, i] = mom[k, i] + push
            work = work + push * vel[k, i]
        energy[i] = work
    stores[3].start()
    stores[4].start()
    for store in stores:
        store.wait()


def local(density, velocity, pressure, species, counts):
    brick = (BX, BY, BZ)
    shape = jax.ShapeDtypeStruct
    anywhere = pl.BlockSpec(memory_space=pl.ANY)
    vmem = pltpu.VMEM
    dma = pltpu.SemaphoreType.DMA
    room = 58 * 1024 * 1024
    table_z, *others = tables()
    gas_shapes = (
        shape(brick, f32),
        shape((3,) + brick, f32),
        shape(brick, f32),
        shape((9,) + brick, f32),
    )
    *gas, waves = pl.pallas_call(
        kernel,
        out_shape=gas_shapes + (shape((3, NZ, 128), f32),),
        in_specs=[anywhere] * 11,
        out_specs=(anywhere,) * 5,
        scratch_shapes=[
            vmem((14, BX + 2, BY, BZ), f32),
            vmem((BX + 2, BY, BZ), f32),
            vmem(brick, f32),
            vmem(brick, jnp.int32),
            vmem((2, NZ, 2 * BZ), bf16),
            vmem((2, NY, NY), bf16),
            vmem((2, 48, 128), bf16),
            vmem((2, 128, 48), bf16),
            vmem((48, NY // 2), f32),
            vmem((BX, 16, NY), f32),
            vmem((14,) + brick, f32),
            vmem((2, NZ, 128), f32),
            vmem((16, 2, 16, 128), f32),
            vmem((128, NY), f32),
            vmem((128, NY), f32),
            vmem((128, 128), f32),
            vmem((128, 128), f32),
            vmem((128, 128), f32),
            vmem((128, 128), f32),
            vmem((8, 3, 16, 128), f32),
            vmem((2, BX, 16, BZ), f32),
            vmem((2, BX, 16, BZ), f32),
            vmem((BX, 8, 128), f32),
            vmem((BX, 8, 128), f32),
            dma((11,)),
            dma((5,)),
            dma((4, 15)),
            dma((4, 15)),
            dma((15,)),
            dma((15,)),
        ],
        compiler_params=pltpu.CompilerParams(
            collective_id=0, has_side_effects=True, vmem_limit_bytes=room
        ),
        name="step",
    )(density, velocity, pressure, species, counts, table_z, *others)
    return pl.pallas_call(
        finish,
        out_shape=gas_shapes + (shape(brick, f32),),
        in_specs=[anywhere] * 8,
        out_specs=(anywhere,) * 5,
        scratch_shapes=[
            vmem(brick, f32),
            vmem((3,) + brick, f32),
            vmem(brick, f32),
            vmem((3,) + brick, f32),
            vmem(brick, f32),
            vmem((9,) + brick, f32),
            vmem((3, NZ, 128), f32),
            vmem((2, NZ, 2 * BZ), bf16),
            vmem((BX + 2, BY, BZ), f32),
            dma((8,)),
            dma((5,)),
        ],
        compiler_params=pltpu.CompilerParams(vmem_limit_bytes=room),
        name="finish",
    )(density, velocity, *gas, waves, table_z)


def solution(mesh):
    in_specs = (
        P("hx", "hy", "ga"),
        P(None, "hx", "hy", "ga"),
        P("hx", "hy", "ga"),
        P(None, "hx", "hy", "ga"),
        P("hx", "hy", "ga"),
    )
    out_specs = (
        P("hx", "hy", "ga"),
        P(None, "hx", "hy", "ga"),
        P("hx", "hy", "ga"),
        P(None, "hx", "hy", "ga"),
        P("hx", "hy", "ga"),
    )
    return jax.shard_map(local, mesh=mesh, in_specs=in_specs, out_specs=out_specs, check_vma=False)
```

```python
import functools

import jax
import jax.numpy as jnp
import ml_dtypes
import numpy as np
from jax import lax
from jax.experimental import pallas as pl
from jax.experimental.pallas import tpu as pltpu
from jax.sharding import PartitionSpec as P

NEWTON = 4
gamma_gas = 5.0 / 3.0
time_step = 0.1
half_step = 0.5 * time_step
cool_rates = (2.0, 5.0, 9.0, 14.0, 20.0, 3.0, 7.0, 11.0, 29.0)
NX, NY, NZ = 128, 256, 256
BX, BY, BZ = 8, 32, 128
MESH = pl.DeviceIdType.MESH
f32 = jnp.float32
bf16 = jnp.bfloat16


def cas_table(length):
    keys = np.arange(length)
    angle = 2.0 * np.pi / length * (keys[:, None] * keys[None, :] % length)
    return np.cos(angle) + np.sin(angle)


def halves(table):
    table = table.astype(np.float32)
    high = table.astype(ml_dtypes.bfloat16)
    low = (table - high.astype(np.float32)).astype(ml_dtypes.bfloat16)
    return np.stack([high, low])


def line_tables():
    blocks = NX // BX
    inner = BX - 1
    lam_y = 4.0 * np.sin(np.pi * np.arange(NY) / NY) ** 2
    lam_z = 4.0 * np.sin(np.pi * np.arange(NZ) / NZ) ** 2
    center = 2.0 + lam_z[:, None] + lam_y[None, :]
    factors = [1.0 / center]
    for _ in range(inner - 1):
        factors.append(1.0 / (center - factors[-1]))
    near = factors[-1]
    far = np.prod(np.stack(factors), axis=0)
    sweep = np.stack(factors + [center], axis=0).reshape(BX, blocks, NZ // blocks, NY)
    waves = np.arange(blocks)
    values = (center - 2.0 * near)[:, None, :] - 2.0 * far[:, None, :] * np.cos(
        2.0 * np.pi * waves / blocks
    )[None, :, None]
    values[0, 0, 0] = 1.0
    inverse = 1.0 / (blocks * values)
    bow = sum((x + 1) * (inner - x) for x in range(inner)) / 2.0
    inverse[0, 0, 0] = bow / (BX * BX * blocks)
    green = np.zeros((NZ, 48, NY // 2))
    green[:, 0:16] = inverse[:, :, 0 : NY // 2]
    green[:, 16:32] = inverse[:, :, NY // 2 :]
    green[0, 32:34, 0] = -1.0 / (BX * blocks)
    table = cas_table(blocks)
    mix = np.zeros((48, blocks, 8))
    spread = np.zeros((blocks, 8, 48))
    for part in range(2):
        rows = slice(16 * part, 16 * part + 16)
        mix[rows, :, 2 * part] = table
        mix[rows, :, 2 * part + 1] = np.roll(table, 1, axis=1)
        spread[:, 2 * part, rows] = np.roll(table, 1, axis=0)
        spread[:, 2 * part + 1, rows] = table
    mix[32, :, 4] = 1.0
    mix[33] = mix[0]
    spread[:, 0:2, 32] = 1.0
    spread[:, 4, 33] = 1.0
    return (
        halves(mix.reshape(48, 8 * blocks)),
        halves(spread.reshape(8 * blocks, 48)),
        green.astype(np.float32),
        np.moveaxis(sweep, 0, 1).astype(np.float32),
    )


def tables():
    table_y = cas_table(NY) / 256.0
    table_z = cas_table(NZ)
    parts = []
    for rank in range(NZ // BZ):
        first = rank * BZ
        edges = np.zeros((NZ, BZ))
        edges[:, 0] = table_z[:, (first - 1) % NZ]
        edges[:, BZ - 1] = table_z[:, (first + BZ) % NZ]
        parts.append(halves(np.concatenate([table_z[:, first : first + BZ], edges], axis=1)))
    return (np.stack(parts), halves(table_y)) + line_tables()


def split(values):
    high = values.astype(bf16)
    return high, (values - high.astype(f32)).astype(bf16)


def dot3(left, right, dims=(((1,), (0,)), ((), ()))):
    def one(i, j):
        return lax.dot_general(left[i], right[j], dims, preferred_element_type=f32)

    return one(0, 0) + (one(0, 1) + one(1, 0))


def swap_chunks(tiles, lane):
    low = lane < 64
    even = (lane // 32) % 2 == 0
    mid = [None] * 4
    for i in range(2):
        mid[i] = jnp.where(low, tiles[i], pltpu.roll(tiles[i + 2], 64, 1))
        mid[i + 2] = jnp.where(low, pltpu.roll(tiles[i], 64, 1), tiles[i + 2])
    out = [None] * 4
    for i in (0, 2):
        out[i] = jnp.where(even, mid[i], pltpu.roll(mid[i + 1], 32, 1))
        out[i + 1] = jnp.where(even, pltpu.roll(mid[i], 96, 1), mid[i + 1])
    return out


def kernel(
    density, velocity, pressure, species, counts, tz_in, ty_in, mix_in, spread_in, green_in, sweep_in,
    o_density, o_momentum, o_energy, o_species, b_buf,
    gas, sound, press, count, tz, ty, mix, spread, green, sweep, out,
    z_src, z_buf, u_buf, d_buf, y_src, x_buf, x_src, w_buf, b_src,
    yp_src, yp_buf, zp_src, zp_buf,
    in_sem, out_sem, send_sem, recv_sem, halo_send, halo_recv,
):
    a = lax.axis_index("hx")
    b = lax.axis_index("hy")
    g = lax.axis_index("ga")
    q = g * 8 + b
    side = lax.rem(g + a, 2)
    chunk = side * 8 + b

    loads = [
        (density, gas.at[0, pl.ds(1, BX)]),
        (tz_in.at[g], tz),
        (velocity, gas.at[pl.ds(1, 3), pl.ds(1, BX)]),
        (species, gas.at[pl.ds(5, 9), pl.ds(1, BX)]),
        (pressure, press),
        (counts, count),
        (ty_in, ty),
        (mix_in, mix),
        (spread_in, spread),
        (green_in.at[chunk * 16 + a], green),
        (sweep_in.at[chunk], sweep),
    ]
    loads = [pltpu.make_async_copy(s, d, in_sem.at[i]) for i, (s, d) in enumerate(loads)]
    for load in loads:
        load.start()

    barrier = pltpu.get_barrier_semaphore()

    def outward(n, middle):
        return middle + ((n + 1) // 2) * (2 * lax.rem(n, 2) - 1)

    def plane_id(n):
        t_b = lax.rem(b + outward(n // 2, 4), 8)
        t_g = lax.rem(g + 1 + n, 2)
        return t_b, t_g, {"hy": t_b, "ga": t_g}

    def line_id(n):
        t = lax.rem(a + outward(n, 8), 16)
        return t, {"hx": t, "ga": lax.rem(side + t, 2)}

    above = {"hx": lax.rem(a + 1, 16)}
    below = {"hx": lax.rem(a + 15, 16)}

    @pl.loop(0, 15)
    def _(n):
        pl.semaphore_signal(barrier, inc=1, device_id=plane_id(n)[2], device_id_type=MESH)
        pl.semaphore_signal(barrier, inc=1, device_id=line_id(n)[1], device_id_type=MESH)

    pl.semaphore_signal(barrier, inc=1, device_id=above, device_id_type=MESH)
    pl.semaphore_signal(barrier, inc=1, device_id=below, device_id_type=MESH)

    def remote(src, dst, sems, slot, target):
        return pltpu.make_async_remote_copy(
            src_ref=src, dst_ref=dst, send_sem=sems[0].at[slot], recv_sem=sems[1].at[slot],
            device_id=target, device_id_type=MESH,
        )

    rounds = [(send_sem.at[r], recv_sem.at[r]) for r in range(4)]

    def send1(n):
        t_b, t_g, where = plane_id(n)
        t = lax.rem(t_g + a, 2) * 8 + t_b
        return remote(z_src.at[:, pl.ds(t * 16, 16)], z_buf.at[q], rounds[0], n, where)

    def send2(n):
        t, where = line_id(n)
        return remote(y_src.at[pl.ds(t * 8, 8)], x_buf.at[pl.ds(a * 8, 8)], rounds[1], n, where)

    def send3(n):
        t, where = line_id(n)
        return remote(x_src.at[pl.ds(t * 8, 8)], w_buf.at[pl.ds(a * 8, 8)], rounds[2], n, where)

    def send4(n):
        t_b, _, where = plane_id(n)
        return remote(b_src.at[t_b], b_buf.at[:, pl.ds(chunk * 16, 16)], rounds[3], n, where)

    def start_all(send):
        @pl.loop(0, 15)
        def _(n):
            send(n).start()

    def arrive_all(send):
        @pl.loop(0, 15)
        def _(n):
            send(n).wait_recv()

    lane16 = lax.broadcasted_iota(jnp.int32, (16, 128), 1)

    loads[0].wait()
    loads[1].wait()
    brick = split(gas[0, pl.ds(1, BX)].reshape(BX * BY, BZ) - 1.0)
    turned = dot3((tz[0, :, 0:BZ], tz[1, :, 0:BZ]), brick, (((1,), (1,)), ((), ())))
    z_src[0] = turned[:, 0:128]
    z_src[1] = turned[:, 128:256]
    pl.semaphore_wait(barrier, 32)
    start_all(send1)
    z_buf[q] = z_src[:, pl.ds(pl.multiple_of(chunk * 16, 16), 16)]

    halos = (halo_send, halo_recv)
    right = {"hy": lax.rem(b + 1, 8)}
    left = {"hy": lax.rem(b + 7, 8)}
    other = {"ga": 1 - g}
    loads[2].wait()
    loads[3].wait()
    face_early = []
    for slot, (first, many) in enumerate(((0, 1), (1, 6), (7, 7))):
        rows = pl.ds(first, many)
        face_early.append(remote(gas.at[rows, BX], gas.at[rows, 0], halos, 9 + 2 * slot, above))
        face_early.append(remote(gas.at[rows, 1], gas.at[rows, BX + 1], halos, 10 + 2 * slot, below))
    for face in face_early[0:2]:
        face.start()
    loads[4].wait()
    loads[5].wait()
    lane8 = lax.broadcasted_iota(jnp.int32, (8, 128), 1)

    def cell_sound(p):
        return jnp.sqrt(gamma_gas * gas[4, p] / gas[0, p])

    @pl.loop(0, BX)
    def _(i):
        p = i + 1
        rho = gas[0, p]
        cooling = cool_rates[0] * gas[5, p]
        for s in range(1, 9):
            cooling = cooling + cool_rates[s] * gas[5 + s, p]
        stiffness = time_step * rho * cooling
        initial = press[i] / ((gamma_gas - 1.0) * rho)
        many = count[i]
        energy = initial
        for step in range(NEWTON):
            near = 1.0 + energy
            square = near * near
            top = (energy - initial) * square + stiffness * energy * energy * near
            bottom = square + stiffness * energy * (energy + 2.0)
            energy = jnp.where(many > step, energy - top / bottom, energy)
        gas[4, p] = (gamma_gas - 1.0) * rho * energy
        sound[p] = jnp.sqrt(gamma_gas * (gamma_gas - 1.0) * energy)
        tile = jnp.zeros((8, 128), f32)
        for f in range(15):
            field = gas[f, p] if f < 14 else sound[p]
            yp_src[0, i, f : f + 1, :] = field[BY - 1 : BY]
            yp_src[1, i, f : f + 1, :] = field[0:1]
            for j in range(4):
                moved = pltpu.roll(field[8 * j : 8 * j + 8], 32 * j + 2 * f + 1, 1)
                tile = jnp.where(lane8 // 2 == 16 * j + f, moved, tile)
        zp_src[i] = tile
        yp_src[0, i, 15:16, :] = jnp.zeros((1, 128), f32)
        yp_src[1, i, 15:16, :] = jnp.zeros((1, 128), f32)

    face_late = [
        remote(yp_src.at[0], yp_buf.at[0], halos, 6, right),
        remote(yp_src.at[1], yp_buf.at[1], halos, 7, left),
        remote(zp_src, zp_buf, halos, 8, other),
    ]

    row32 = lax.broadcasted_iota(jnp.int32, (BY, BZ), 0)
    lane32 = lax.broadcasted_iota(jnp.int32, (BY, BZ), 1)

    def hydro(i):
        p = i + 1

        def at(f, where):
            return gas[f, where] if f < 14 else sound[where]

        def sides(f, d):
            if d == 0:
                return at(f, p - 1), at(f, p + 1)
            field = at(f, p)
            if d == 1:
                lower = jnp.where(row32 == 0, yp_buf[0, i, f : f + 1, :], pltpu.roll(field, 1, 0))
                upper = jnp.where(
                    row32 == BY - 1, yp_buf[1, i, f : f + 1, :], pltpu.roll(field, BY - 1, 0)
                )
                return lower, upper
            tile = zp_buf[i]
            edge = jnp.concatenate(
                [pltpu.roll(tile, (BZ - 1 - 32 * j - 2 * f) % 128, 1) for j in range(4)], axis=0
            )
            lower = pltpu.roll(jnp.where(lane32 == BZ - 1, edge, field), 1, 1)
            upper = pltpu.roll(jnp.where(lane32 == 0, edge, field), BZ - 1, 1)
            return lower, upper

        rho = gas[0, p]
        vel = [gas[1 + k, p] for k in range(3)]
        cs = sound[p]
        keep = 1.0
        weights = []
        new_rho = 0.0
        new_energy = 0.0
        new_mom = [0.0, 0.0, 0.0]
        for d in range(3):
            rho_l, rho_u = sides(0, d)
            v_l, v_u = zip(*[sides(1 + k, d) for k in range(3)])
            p_l, p_u = sides(4, d)
            c_l, c_u = sides(14, d)
            here = jnp.abs(vel[d]) + cs
            w_l = jnp.maximum(here, jnp.abs(v_l[d]) + c_l)
            w_u = jnp.maximum(here, jnp.abs(v_u[d]) + c_u)
            b_l = half_step * (w_l + v_l[d])
            b_u = half_step * (w_u - v_u[d])
            a_l = b_l * rho_l
            a_u = b_u * rho_u
            keep = keep - half_step * (w_l + w_u)
            weights.append((a_l, a_u))
            new_rho = new_rho + (a_l + a_u)
            for k in range(3):
                new_mom[k] = new_mom[k] + (a_l * v_l[k] + a_u * v_u[k])
            new_mom[d] = new_mom[d] + half_step * (p_l - p_u)
            sq_l = v_l[0] * v_l[0] + v_l[1] * v_l[1] + v_l[2] * v_l[2]
            sq_u = v_u[0] * v_u[0] + v_u[1] * v_u[1] + v_u[2] * v_u[2]
            new_energy = new_energy + (
                0.5 * (a_l * sq_l + a_u * sq_u)
                + p_l * (1.5 * b_l + half_step * v_l[d])
                + p_u * (1.5 * b_u - half_step * v_u[d])
            )
        mass = keep * rho
        out[0, i] = new_rho + mass
        for k in range(3):
            out[1 + k, i] = new_mom[k] + mass * vel[k]
        sq = vel[0] * vel[0] + vel[1] * vel[1] + vel[2] * vel[2]
        out[4, i] = new_energy + keep * (1.5 * gas[4, p]) + 0.5 * mass * sq
        for s in range(5, 14):
            result = mass * gas[s, p]
            for d in range(3):
                lower, upper = sides(s, d)
                result = result + (weights[d][0] * lower + weights[d][1] * upper)
            out[s, i] = result

    loads[6].wait()
    arrive_all(send1)
    for hi in range(2):
        for xh in range(2):
            tiles = [z_buf[4 * hi + i, xh] + z_buf[8 + 4 * hi + i, xh] for i in range(4)]
            tiles = swap_chunks(tiles, lane16)
            for xl in range(4):
                x = 4 * xh + xl
                u_buf[16 * x : 16 * x + 16, 128 * hi : 128 * hi + 128] = tiles[xl]
    table_y = (ty[0], ty[1])
    d_buf[...] = dot3(split(u_buf[...]), table_y)

    for load in loads[7:]:
        load.wait()

    def plane(x):
        return d_buf[16 * x : 16 * x + 16, :]

    def inside(before, after, mean):
        values = []
        carry = before
        for x in range(BX - 1):
            carry = carry + (mean - plane(x))
            if x == BX - 2:
                carry = carry + after
            carry = carry * sweep[x]
            values.append(carry)
        for x in range(BX - 3, -1, -1):
            values[x] = values[x] + sweep[x] * values[x + 1]
        return values

    values = inside(0.0, 0.0, 0.0)
    last = values[BX - 2] - plane(BX - 1)
    first = values[0]
    whole = functools.reduce(lambda p, r: p + r, [v[:, 0:128] for v in values])
    y_src[...] = jnp.zeros((128, 128), f32)
    for r, row in enumerate((last[:, 0:128], first[:, 0:128], last[:, 128:], first[:, 128:], whole)):
        y_src[pl.ds(r, 16, stride=8), :] = row
    start_all(send2)
    for face in face_late:
        face.start()
    for face in face_early[2:4]:
        face.start()
    x_buf[pl.ds(pl.multiple_of(a * 8, 8), 8)] = y_src[pl.ds(pl.multiple_of(a * 8, 8), 8)]

    arrive_all(send2)
    waves = dot3((mix[0], mix[1]), split(x_buf[...])) * green[...]
    x_src[...] = dot3((spread[0], spread[1]), split(waves))
    start_all(send3)
    for face in face_early[4:6]:
        face.start()
    w_buf[pl.ds(pl.multiple_of(a * 8, 8), 8)] = x_src[pl.ds(pl.multiple_of(a * 8, 8), 8)]

    for face in face_late[0:3]:
        face.wait_recv()

    @pl.loop(1, 7)
    def _(i):
        hydro(i)


    arrive_all(send3)

    def returned(r):
        return w_buf[pl.ds(r, 16, stride=8), :]

    before = jnp.concatenate([returned(0), returned(2)], axis=1)
    own_plane = jnp.concatenate([returned(1), returned(3)], axis=1)
    mean = returned(4)
    mean = jnp.concatenate([mean, jnp.zeros_like(mean)], axis=1)
    values = inside(before, own_plane, mean)
    beyond = sweep[BX - 1] * own_plane - values[BX - 2] + (plane(BX - 1) - mean)
    back = dot3(split(jnp.concatenate(values + [own_plane, before, beyond], axis=0)), table_y)

    def line(hi, row):
        return back[16 * row : 16 * row + 16, 128 * hi : 128 * hi + 128]

    spot = lane16 % 32
    for hi in range(2):
        rows_low = jnp.zeros((16, 128), f32)
        rows_high = rows_low
        for xh in range(2):
            tiles = [line(hi, 4 * xh + xl) for xl in range(4)]
            outer = [line(1 - hi, 4 * xh + xl) for xl in range(4)]
            for xl in range(4):
                x = 4 * xh + xl
                low = jnp.where(
                    lane16 < 32, pltpu.roll(outer[xl], 1 + x, 1), pltpu.roll(tiles[xl], 1 + x, 1)
                )
                high = jnp.where(
                    lane16 >= 96, pltpu.roll(outer[xl], 96 + x, 1), pltpu.roll(tiles[xl], 96 + x, 1)
                )
                rows_low = jnp.where(spot == x, low, rows_low)
                rows_high = jnp.where(spot == x, high, rows_high)
            tiles = swap_chunks(tiles, lane16)
            for i in range(4):
                b_src[4 * hi + i, xh] = tiles[i]
        tiles = swap_chunks([line(hi, 8), line(hi, 9), rows_low, rows_high], lane16)
        for i in range(4):
            b_src[4 * hi + i, 2] = tiles[i]
    start_all(send4)
    own = pltpu.make_async_copy(b_src.at[b], b_buf.at[:, pl.ds(chunk * 16, 16)], out_sem.at[4])
    own.start()

    for face in face_early:
        face.wait_recv()
    sound[0] = cell_sound(0)
    sound[BX + 1] = cell_sound(BX + 1)

    @pl.loop(0, 2)
    def _(i):
        hydro(i * (BX - 1))

    stores = [
        own,
        pltpu.make_async_copy(out.at[0], o_density, out_sem.at[0]),
        pltpu.make_async_copy(out.at[pl.ds(1, 3)], o_momentum, out_sem.at[1]),
        pltpu.make_async_copy(out.at[4], o_energy, out_sem.at[2]),
        pltpu.make_async_copy(out.at[pl.ds(5, 9)], o_species, out_sem.at[3]),
    ]
    for store in stores[1:]:
        store.start()

    for send in (send1, send2, send3, send4):

        @pl.loop(0, 15)
        def _(n):
            send(n).wait_send()

    for face in face_early + face_late:
        face.wait_send()
    for store in stores:
        store.wait()
    arrive_all(send4)


def finish(
    density, velocity, density_in, momentum_in, energy_in, species_in, waves, tz_in,
    o_density, o_momentum, o_energy, o_species, o_potential,
    rho, vel, new_rho, mom, energy, frac, spec, tz, pot, load_sem, store_sem,
):
    loads = [
        (waves, spec),
        (tz_in.at[lax.axis_index("ga")], tz),
        (density_in, new_rho),
        (species_in, frac),
        (density, rho),
        (velocity, vel),
        (momentum_in, mom),
        (energy_in, energy),
    ]
    loads = [pltpu.make_async_copy(s, d, load_sem.at[i]) for i, (s, d) in enumerate(loads)]
    stores = [
        (new_rho, o_density),
        (frac, o_species),
        (pot.at[pl.ds(1, BX)], o_potential),
        (mom.at[:, pl.ds(0, 4)], o_momentum.at[:, pl.ds(0, 4)]),
        (energy.at[pl.ds(0, 4)], o_energy.at[pl.ds(0, 4)]),
        (mom.at[:, pl.ds(4, 4)], o_momentum.at[:, pl.ds(4, 4)]),
        (energy.at[pl.ds(4, 4)], o_energy.at[pl.ds(4, 4)]),
    ]
    stores = [pltpu.make_async_copy(s, d, store_sem.at[i]) for i, (s, d) in enumerate(stores)]
    for load in loads:
        load.start()
    loads[0].wait()
    loads[1].wait()
    table = (tz[0], tz[1])
    edges = []
    for xh in range(2):
        done = dot3(split(spec[xh].T), table)
        edges.append(done[:, BZ:])
        for xl in range(4):
            pot[1 + 4 * xh + xl] = done[32 * xl : 32 * xl + 32, 0:BZ]
    stores[2].start()
    done = dot3(split(spec[2].T), (tz[0, :, 0:BZ], tz[1, :, 0:BZ]))
    pot[0] = done[0:32]
    pot[BX + 1] = done[32:64]
    for i in range(2):
        loads[2 + i].wait()
        stores[i].start()
    for load in loads[4:]:
        load.wait()
    row32 = lax.broadcasted_iota(jnp.int32, (BY, BZ), 0)
    lane32 = lax.broadcasted_iota(jnp.int32, (BY, BZ), 1)
    for i in range(BX):
        here = pot[1 + i]
        edge = edges[i // 4][32 * (i % 4) : 32 * (i % 4) + 32]
        pull = [
            pot[i] - pot[i + 2],
            jnp.where(row32 == 0, done[64 + i : 65 + i], pltpu.roll(here, 1, 0))
            - jnp.where(row32 == BY - 1, done[96 + i : 97 + i], pltpu.roll(here, BY - 1, 0)),
            jnp.where(lane32 == 0, edge, pltpu.roll(here, 1, 1))
            - jnp.where(lane32 == BZ - 1, edge, pltpu.roll(here, BZ - 1, 1)),
        ]
        weight = half_step * rho[i]
        work = energy[i]
        for k in range(3):
            push = weight * pull[k]
            mom[k, i] = mom[k, i] + push
            work = work + push * vel[k, i]
        energy[i] = work
        if i == 3:
            stores[3].start()
            stores[4].start()
    stores[5].start()
    stores[6].start()
    for store in stores:
        store.wait()


def local(density, velocity, pressure, species, counts):
    brick = (BX, BY, BZ)
    shape = jax.ShapeDtypeStruct
    anywhere = pl.BlockSpec(memory_space=pl.ANY)
    vmem = pltpu.VMEM
    dma = pltpu.SemaphoreType.DMA
    room = 58 * 1024 * 1024
    table_z, *others = tables()
    gas_shapes = (
        shape(brick, f32),
        shape((3,) + brick, f32),
        shape(brick, f32),
        shape((9,) + brick, f32),
    )
    *gas, waves = pl.pallas_call(
        kernel,
        out_shape=gas_shapes + (shape((3, NZ, 128), f32),),
        in_specs=[anywhere] * 11,
        out_specs=(anywhere,) * 5,
        scratch_shapes=[
            vmem((14, BX + 2, BY, BZ), f32),
            vmem((BX + 2, BY, BZ), f32),
            vmem(brick, f32),
            vmem(brick, jnp.int32),
            vmem((2, NZ, 2 * BZ), bf16),
            vmem((2, NY, NY), bf16),
            vmem((2, 48, 128), bf16),
            vmem((2, 128, 48), bf16),
            vmem((48, NY // 2), f32),
            vmem((BX, 16, NY), f32),
            vmem((14,) + brick, f32),
            vmem((2, NZ, 128), f32),
            vmem((16, 2, 16, 128), f32),
            vmem((128, NY), f32),
            vmem((128, NY), f32),
            vmem((128, 128), f32),
            vmem((128, 128), f32),
            vmem((128, 128), f32),
            vmem((128, 128), f32),
            vmem((8, 3, 16, 128), f32),
            vmem((2, BX, 16, BZ), f32),
            vmem((2, BX, 16, BZ), f32),
            vmem((BX, 8, 128), f32),
            vmem((BX, 8, 128), f32),
            dma((11,)),
            dma((5,)),
            dma((4, 15)),
            dma((4, 15)),
            dma((15,)),
            dma((15,)),
        ],
        compiler_params=pltpu.CompilerParams(
            collective_id=0, has_side_effects=True, vmem_limit_bytes=room
        ),
        name="step",
    )(density, velocity, pressure, species, counts, table_z, *others)
    return pl.pallas_call(
        finish,
        out_shape=gas_shapes + (shape(brick, f32),),
        in_specs=[anywhere] * 8,
        out_specs=(anywhere,) * 5,
        scratch_shapes=[
            vmem(brick, f32),
            vmem((3,) + brick, f32),
            vmem(brick, f32),
            vmem((3,) + brick, f32),
            vmem(brick, f32),
            vmem((9,) + brick, f32),
            vmem((3, NZ, 128), f32),
            vmem((2, NZ, 2 * BZ), bf16),
            vmem((BX + 2, BY, BZ), f32),
            dma((8,)),
            dma((7,)),
        ],
        compiler_params=pltpu.CompilerParams(vmem_limit_bytes=room),
        name="finish",
    )(density, velocity, *gas, waves, table_z)


def solution(mesh):
    in_specs = (
        P("hx", "hy", "ga"),
        P(None, "hx", "hy", "ga"),
        P("hx", "hy", "ga"),
        P(None, "hx", "hy", "ga"),
        P("hx", "hy", "ga"),
    )
    out_specs = (
        P("hx", "hy", "ga"),
        P(None, "hx", "hy", "ga"),
        P("hx", "hy", "ga"),
        P(None, "hx", "hy", "ga"),
        P("hx", "hy", "ga"),
    )
    return jax.shard_map(local, mesh=mesh, in_specs=in_specs, out_specs=out_specs, check_vma=False)
```

```python
import functools

import jax
import jax.numpy as jnp
import ml_dtypes
import numpy as np
from jax import lax
from jax.experimental import pallas as pl
from jax.experimental.pallas import tpu as pltpu
from jax.sharding import PartitionSpec as P

NEWTON = 4
gamma_gas = 5.0 / 3.0
time_step = 0.1
half_step = 0.5 * time_step
cool_rates = (2.0, 5.0, 9.0, 14.0, 20.0, 3.0, 7.0, 11.0, 29.0)
NX, NY, NZ = 128, 256, 256
BX, BY, BZ = 8, 32, 128
MESH = pl.DeviceIdType.MESH
f32 = jnp.float32
bf16 = jnp.bfloat16


def cas_table(length):
    keys = np.arange(length)
    angle = 2.0 * np.pi / length * (keys[:, None] * keys[None, :] % length)
    return np.cos(angle) + np.sin(angle)


def halves(table):
    table = table.astype(np.float32)
    high = table.astype(ml_dtypes.bfloat16)
    low = (table - high.astype(np.float32)).astype(ml_dtypes.bfloat16)
    return np.stack([high, low])


def line_tables():
    blocks = NX // BX
    inner = BX - 1
    lam_y = 4.0 * np.sin(np.pi * np.arange(NY) / NY) ** 2
    lam_z = 4.0 * np.sin(np.pi * np.arange(NZ) / NZ) ** 2
    center = 2.0 + lam_z[:, None] + lam_y[None, :]
    factors = [1.0 / center]
    for _ in range(inner - 1):
        factors.append(1.0 / (center - factors[-1]))
    near = factors[-1]
    far = np.prod(np.stack(factors), axis=0)
    sweep = np.stack(factors + [center], axis=0).reshape(BX, blocks, NZ // blocks, NY)
    waves = np.arange(blocks)
    values = (center - 2.0 * near)[:, None, :] - 2.0 * far[:, None, :] * np.cos(
        2.0 * np.pi * waves / blocks
    )[None, :, None]
    values[0, 0, 0] = 1.0
    inverse = 1.0 / (blocks * values)
    bow = sum((x + 1) * (inner - x) for x in range(inner)) / 2.0
    inverse[0, 0, 0] = bow / (BX * BX * blocks)
    green = np.zeros((NZ, 48, NY // 2))
    green[:, 0:16] = inverse[:, :, 0 : NY // 2]
    green[:, 16:32] = inverse[:, :, NY // 2 :]
    green[0, 32:34, 0] = -1.0 / (BX * blocks)
    table = cas_table(blocks)
    mix = np.zeros((48, blocks, 8))
    spread = np.zeros((blocks, 8, 48))
    for part in range(2):
        rows = slice(16 * part, 16 * part + 16)
        mix[rows, :, 2 * part] = table
        mix[rows, :, 2 * part + 1] = np.roll(table, 1, axis=1)
        spread[:, 2 * part, rows] = np.roll(table, 1, axis=0)
        spread[:, 2 * part + 1, rows] = table
    mix[32, :, 4] = 1.0
    mix[33] = mix[0]
    spread[:, 0:2, 32] = 1.0
    spread[:, 4, 33] = 1.0
    return (
        halves(mix.reshape(48, 8 * blocks)),
        halves(spread.reshape(8 * blocks, 48)),
        green.astype(np.float32),
        np.moveaxis(sweep, 0, 1).astype(np.float32),
    )


def tables():
    table_y = cas_table(NY) / 256.0
    table_z = cas_table(NZ)
    parts = []
    for rank in range(NZ // BZ):
        first = rank * BZ
        edges = np.zeros((NZ, BZ))
        edges[:, 0] = table_z[:, (first - 1) % NZ]
        edges[:, BZ - 1] = table_z[:, (first + BZ) % NZ]
        parts.append(halves(np.concatenate([table_z[:, first : first + BZ], edges], axis=1)))
    return (np.stack(parts), halves(table_y)) + line_tables()


def split(values):
    high = values.astype(bf16)
    return high, (values - high.astype(f32)).astype(bf16)


def dot3(left, right, dims=(((1,), (0,)), ((), ()))):
    def one(i, j):
        return lax.dot_general(left[i], right[j], dims, preferred_element_type=f32)

    return one(0, 0) + (one(0, 1) + one(1, 0))


def swap_chunks(tiles, lane):
    low = lane < 64
    even = (lane // 32) % 2 == 0
    mid = [None] * 4
    for i in range(2):
        mid[i] = jnp.where(low, tiles[i], pltpu.roll(tiles[i + 2], 64, 1))
        mid[i + 2] = jnp.where(low, pltpu.roll(tiles[i], 64, 1), tiles[i + 2])
    out = [None] * 4
    for i in (0, 2):
        out[i] = jnp.where(even, mid[i], pltpu.roll(mid[i + 1], 32, 1))
        out[i + 1] = jnp.where(even, pltpu.roll(mid[i], 96, 1), mid[i + 1])
    return out


def kernel(
    density, velocity, pressure, species, counts, tz_in, ty_in, mix_in, spread_in, green_in, sweep_in,
    o_density, o_momentum, o_energy, o_species, b_buf,
    gas, sound, press, count, tz, ty, mix, spread, green, sweep, out,
    z_src, z_buf, u_buf, d_buf, y_src, x_buf, x_src, w_buf, b_src,
    yp_src, yp_buf, zp_src, zp_buf,
    in_sem, out_sem, send_sem, recv_sem, halo_send, halo_recv,
):
    a = lax.axis_index("hx")
    b = lax.axis_index("hy")
    g = lax.axis_index("ga")
    q = g * 8 + b
    side = lax.rem(g + a, 2)
    chunk = side * 8 + b

    loads = [
        (density, gas.at[0, pl.ds(1, BX)]),
        (tz_in.at[g], tz),
        (velocity, gas.at[pl.ds(1, 3), pl.ds(1, BX)]),
        (species, gas.at[pl.ds(5, 9), pl.ds(1, BX)]),
        (pressure, press),
        (counts, count),
        (ty_in, ty),
        (mix_in, mix),
        (spread_in, spread),
        (green_in.at[chunk * 16 + a], green),
        (sweep_in.at[chunk], sweep),
    ]
    loads = [pltpu.make_async_copy(s, d, in_sem.at[i]) for i, (s, d) in enumerate(loads)]
    for load in loads:
        load.start()

    barrier = pltpu.get_barrier_semaphore()

    def outward(n, middle):
        return middle + ((n + 1) // 2) * (2 * lax.rem(n, 2) - 1)

    def plane_id(n):
        t_b = lax.rem(b + outward(n // 2, 4), 8)
        t_g = lax.rem(g + 1 + n, 2)
        return t_b, t_g, {"hy": t_b, "ga": t_g}

    def line_id(n):
        t = lax.rem(a + outward(n, 8), 16)
        return t, {"hx": t, "ga": lax.rem(side + t, 2)}

    above = {"hx": lax.rem(a + 1, 16)}
    below = {"hx": lax.rem(a + 15, 16)}

    @pl.loop(0, 15)
    def _(n):
        pl.semaphore_signal(barrier, inc=1, device_id=plane_id(n)[2], device_id_type=MESH)
        pl.semaphore_signal(barrier, inc=1, device_id=line_id(n)[1], device_id_type=MESH)

    pl.semaphore_signal(barrier, inc=1, device_id=above, device_id_type=MESH)
    pl.semaphore_signal(barrier, inc=1, device_id=below, device_id_type=MESH)

    def remote(src, dst, sems, slot, target):
        return pltpu.make_async_remote_copy(
            src_ref=src, dst_ref=dst, send_sem=sems[0].at[slot], recv_sem=sems[1].at[slot],
            device_id=target, device_id_type=MESH,
        )

    rounds = [(send_sem.at[r], recv_sem.at[r]) for r in range(4)]

    def send1(n):
        t_b, t_g, where = plane_id(n)
        t = lax.rem(t_g + a, 2) * 8 + t_b
        return remote(z_src.at[t], z_buf.at[q], rounds[0], n, where)

    def send2(n):
        t, where = line_id(n)
        return remote(y_src.at[pl.ds(t * 8, 8)], x_buf.at[pl.ds(a * 8, 8)], rounds[1], n, where)

    def send3(n):
        t, where = line_id(n)
        return remote(x_src.at[pl.ds(t * 8, 8)], w_buf.at[pl.ds(a * 8, 8)], rounds[2], n, where)

    def send4(n):
        t_b, _, where = plane_id(n)
        return remote(b_src.at[t_b], b_buf.at[chunk], rounds[3], n, where)

    def start_all(send):
        @pl.loop(0, 15)
        def _(n):
            send(n).start()

    def arrive_all(send):
        @pl.loop(0, 15)
        def _(n):
            send(n).wait_recv()

    lane16 = lax.broadcasted_iota(jnp.int32, (16, 128), 1)

    loads[0].wait()
    loads[1].wait()
    brick = split(gas[0, pl.ds(1, BX)].reshape(BX * BY, BZ) - 1.0)
    turned = dot3((tz[0, :, 0:BZ], tz[1, :, 0:BZ]), brick, (((1,), (1,)), ((), ())))
    z_src[:, 0] = turned[:, 0:128].reshape(16, 16, 128)
    z_src[:, 1] = turned[:, 128:256].reshape(16, 16, 128)
    pl.semaphore_wait(barrier, 32)
    start_all(send1)
    z_buf[q] = z_src[chunk]

    halos = (halo_send, halo_recv)
    right = {"hy": lax.rem(b + 1, 8)}
    left = {"hy": lax.rem(b + 7, 8)}
    other = {"ga": 1 - g}
    loads[2].wait()
    loads[3].wait()
    face_early = []
    for slot, (first, many) in enumerate(((0, 1), (1, 6), (7, 7))):
        rows = pl.ds(first, many)
        face_early.append(remote(gas.at[rows, BX], gas.at[rows, 0], halos, 9 + 2 * slot, above))
        face_early.append(remote(gas.at[rows, 1], gas.at[rows, BX + 1], halos, 10 + 2 * slot, below))
    for face in face_early[0:2]:
        face.start()
    loads[4].wait()
    loads[5].wait()
    lane8 = lax.broadcasted_iota(jnp.int32, (8, 128), 1)

    def cell_sound(p):
        return jnp.sqrt(gamma_gas * gas[4, p] / gas[0, p])

    @pl.loop(0, BX)
    def _(i):
        p = i + 1
        rho = gas[0, p]
        cooling = cool_rates[0] * gas[5, p]
        for s in range(1, 9):
            cooling = cooling + cool_rates[s] * gas[5 + s, p]
        stiffness = time_step * rho * cooling
        initial = press[i] / ((gamma_gas - 1.0) * rho)
        many = count[i]
        energy = initial
        for step in range(NEWTON):
            near = 1.0 + energy
            square = near * near
            top = (energy - initial) * square + stiffness * energy * energy * near
            bottom = square + stiffness * energy * (energy + 2.0)
            energy = jnp.where(many > step, energy - top / bottom, energy)
        gas[4, p] = (gamma_gas - 1.0) * rho * energy
        sound[p] = jnp.sqrt(gamma_gas * (gamma_gas - 1.0) * energy)
        tile = jnp.zeros((8, 128), f32)
        for f in range(15):
            field = gas[f, p] if f < 14 else sound[p]
            yp_src[0, i, f : f + 1, :] = field[BY - 1 : BY]
            yp_src[1, i, f : f + 1, :] = field[0:1]
            for j in range(4):
                moved = pltpu.roll(field[8 * j : 8 * j + 8], 32 * j + 2 * f + 1, 1)
                tile = jnp.where(lane8 // 2 == 16 * j + f, moved, tile)
        zp_src[i] = tile
        yp_src[0, i, 15:16, :] = jnp.zeros((1, 128), f32)
        yp_src[1, i, 15:16, :] = jnp.zeros((1, 128), f32)

    face_late = [
        remote(yp_src.at[0], yp_buf.at[0], halos, 6, right),
        remote(yp_src.at[1], yp_buf.at[1], halos, 7, left),
        remote(zp_src, zp_buf, halos, 8, other),
    ]

    row32 = lax.broadcasted_iota(jnp.int32, (BY, BZ), 0)
    lane32 = lax.broadcasted_iota(jnp.int32, (BY, BZ), 1)

    def hydro(i):
        p = i + 1

        def at(f, where):
            return gas[f, where] if f < 14 else sound[where]

        def sides(f, d):
            if d == 0:
                return at(f, p - 1), at(f, p + 1)
            field = at(f, p)
            if d == 1:
                lower = jnp.where(row32 == 0, yp_buf[0, i, f : f + 1, :], pltpu.roll(field, 1, 0))
                upper = jnp.where(
                    row32 == BY - 1, yp_buf[1, i, f : f + 1, :], pltpu.roll(field, BY - 1, 0)
                )
                return lower, upper
            tile = zp_buf[i]
            edge = jnp.concatenate(
                [pltpu.roll(tile, (BZ - 1 - 32 * j - 2 * f) % 128, 1) for j in range(4)], axis=0
            )
            lower = pltpu.roll(jnp.where(lane32 == BZ - 1, edge, field), 1, 1)
            upper = pltpu.roll(jnp.where(lane32 == 0, edge, field), BZ - 1, 1)
            return lower, upper

        rho = gas[0, p]
        vel = [gas[1 + k, p] for k in range(3)]
        cs = sound[p]
        keep = 1.0
        weights = []
        new_rho = 0.0
        new_energy = 0.0
        new_mom = [0.0, 0.0, 0.0]
        for d in range(3):
            rho_l, rho_u = sides(0, d)
            v_l, v_u = zip(*[sides(1 + k, d) for k in range(3)])
            p_l, p_u = sides(4, d)
            c_l, c_u = sides(14, d)
            here = jnp.abs(vel[d]) + cs
            w_l = jnp.maximum(here, jnp.abs(v_l[d]) + c_l)
            w_u = jnp.maximum(here, jnp.abs(v_u[d]) + c_u)
            b_l = half_step * (w_l + v_l[d])
            b_u = half_step * (w_u - v_u[d])
            a_l = b_l * rho_l
            a_u = b_u * rho_u
            keep = keep - half_step * (w_l + w_u)
            weights.append((a_l, a_u))
            new_rho = new_rho + (a_l + a_u)
            for k in range(3):
                new_mom[k] = new_mom[k] + (a_l * v_l[k] + a_u * v_u[k])
            new_mom[d] = new_mom[d] + half_step * (p_l - p_u)
            sq_l = v_l[0] * v_l[0] + v_l[1] * v_l[1] + v_l[2] * v_l[2]
            sq_u = v_u[0] * v_u[0] + v_u[1] * v_u[1] + v_u[2] * v_u[2]
            new_energy = new_energy + (
                0.5 * (a_l * sq_l + a_u * sq_u)
                + p_l * (1.5 * b_l + half_step * v_l[d])
                + p_u * (1.5 * b_u - half_step * v_u[d])
            )
        mass = keep * rho
        out[0, i] = new_rho + mass
        for k in range(3):
            out[1 + k, i] = new_mom[k] + mass * vel[k]
        sq = vel[0] * vel[0] + vel[1] * vel[1] + vel[2] * vel[2]
        out[4, i] = new_energy + keep * (1.5 * gas[4, p]) + 0.5 * mass * sq
        for s in range(5, 14):
            result = mass * gas[s, p]
            for d in range(3):
                lower, upper = sides(s, d)
                result = result + (weights[d][0] * lower + weights[d][1] * upper)
            out[s, i] = result

    loads[6].wait()
    arrive_all(send1)
    for hi in range(2):
        for xh in range(2):
            tiles = [z_buf[4 * hi + i, xh] + z_buf[8 + 4 * hi + i, xh] for i in range(4)]
            tiles = swap_chunks(tiles, lane16)
            for xl in range(4):
                x = 4 * xh + xl
                u_buf[16 * x : 16 * x + 16, 128 * hi : 128 * hi + 128] = tiles[xl]
    table_y = (ty[0], ty[1])
    d_buf[...] = dot3(split(u_buf[...]), table_y)

    for load in loads[7:]:
        load.wait()

    def plane(x):
        return d_buf[16 * x : 16 * x + 16, :]

    def inside(before, after, mean):
        values = []
        carry = before
        for x in range(BX - 1):
            carry = carry + (mean - plane(x))
            if x == BX - 2:
                carry = carry + after
            carry = carry * sweep[x]
            values.append(carry)
        for x in range(BX - 3, -1, -1):
            values[x] = values[x] + sweep[x] * values[x + 1]
        return values

    values = inside(0.0, 0.0, 0.0)
    last = values[BX - 2] - plane(BX - 1)
    first = values[0]
    whole = functools.reduce(lambda p, r: p + r, [v[:, 0:128] for v in values])
    y_src[...] = jnp.zeros((128, 128), f32)
    for r, row in enumerate((last[:, 0:128], first[:, 0:128], last[:, 128:], first[:, 128:], whole)):
        y_src[pl.ds(r, 16, stride=8), :] = row
    start_all(send2)
    for face in face_late:
        face.start()
    for face in face_early[2:4]:
        face.start()
    x_buf[pl.ds(pl.multiple_of(a * 8, 8), 8)] = y_src[pl.ds(pl.multiple_of(a * 8, 8), 8)]

    arrive_all(send2)
    waves = dot3((mix[0], mix[1]), split(x_buf[...])) * green[...]
    x_src[...] = dot3((spread[0], spread[1]), split(waves))
    start_all(send3)
    for face in face_early[4:6]:
        face.start()
    w_buf[pl.ds(pl.multiple_of(a * 8, 8), 8)] = x_src[pl.ds(pl.multiple_of(a * 8, 8), 8)]

    for face in face_late[0:3]:
        face.wait_recv()

    @pl.loop(1, 7)
    def _(i):
        hydro(i)


    arrive_all(send3)

    def returned(r):
        return w_buf[pl.ds(r, 16, stride=8), :]

    before = jnp.concatenate([returned(0), returned(2)], axis=1)
    own_plane = jnp.concatenate([returned(1), returned(3)], axis=1)
    mean = returned(4)
    mean = jnp.concatenate([mean, jnp.zeros_like(mean)], axis=1)
    values = inside(before, own_plane, mean)
    beyond = sweep[BX - 1] * own_plane - values[BX - 2] + (plane(BX - 1) - mean)
    back = dot3(split(jnp.concatenate(values + [own_plane, before, beyond], axis=0)), table_y)

    def line(hi, row):
        return back[16 * row : 16 * row + 16, 128 * hi : 128 * hi + 128]

    spot = lane16 % 32
    for hi in range(2):
        rows_low = jnp.zeros((16, 128), f32)
        rows_high = rows_low
        for xh in range(2):
            tiles = [line(hi, 4 * xh + xl) for xl in range(4)]
            outer = [line(1 - hi, 4 * xh + xl) for xl in range(4)]
            for xl in range(4):
                x = 4 * xh + xl
                low = jnp.where(
                    lane16 < 32, pltpu.roll(outer[xl], 1 + x, 1), pltpu.roll(tiles[xl], 1 + x, 1)
                )
                high = jnp.where(
                    lane16 >= 96, pltpu.roll(outer[xl], 96 + x, 1), pltpu.roll(tiles[xl], 96 + x, 1)
                )
                rows_low = jnp.where(spot == x, low, rows_low)
                rows_high = jnp.where(spot == x, high, rows_high)
            tiles = swap_chunks(tiles, lane16)
            for i in range(4):
                b_src[4 * hi + i, xh] = tiles[i]
        tiles = swap_chunks([line(hi, 8), line(hi, 9), rows_low, rows_high], lane16)
        for i in range(4):
            b_src[4 * hi + i, 2] = tiles[i]
    start_all(send4)
    own = pltpu.make_async_copy(b_src.at[b], b_buf.at[chunk], out_sem.at[4])
    own.start()

    for face in face_early:
        face.wait_recv()
    sound[0] = cell_sound(0)
    sound[BX + 1] = cell_sound(BX + 1)

    @pl.loop(0, 2)
    def _(i):
        hydro(i * (BX - 1))

    stores = [
        own,
        pltpu.make_async_copy(out.at[0], o_density, out_sem.at[0]),
        pltpu.make_async_copy(out.at[pl.ds(1, 3)], o_momentum, out_sem.at[1]),
        pltpu.make_async_copy(out.at[4], o_energy, out_sem.at[2]),
        pltpu.make_async_copy(out.at[pl.ds(5, 9)], o_species, out_sem.at[3]),
    ]
    for store in stores[1:]:
        store.start()

    for send in (send1, send2, send3, send4):

        @pl.loop(0, 15)
        def _(n):
            send(n).wait_send()

    for face in face_early + face_late:
        face.wait_send()
    for store in stores:
        store.wait()
    arrive_all(send4)


def finish(
    density, velocity, density_in, momentum_in, energy_in, species_in, waves, tz_in,
    o_density, o_momentum, o_energy, o_species, o_potential,
    rho, vel, new_rho, mom, energy, frac, spec, tz, pot, load_sem, store_sem,
):
    loads = [
        (waves, spec),
        (tz_in.at[lax.axis_index("ga")], tz),
        (density_in, new_rho),
        (species_in, frac),
        (density, rho),
        (velocity, vel),
        (momentum_in, mom),
        (energy_in, energy),
    ]
    loads = [pltpu.make_async_copy(s, d, load_sem.at[i]) for i, (s, d) in enumerate(loads)]
    stores = [
        (new_rho, o_density),
        (frac, o_species),
        (pot.at[pl.ds(1, BX)], o_potential),
        (mom.at[:, pl.ds(0, 4)], o_momentum.at[:, pl.ds(0, 4)]),
        (energy.at[pl.ds(0, 4)], o_energy.at[pl.ds(0, 4)]),
        (mom.at[:, pl.ds(4, 4)], o_momentum.at[:, pl.ds(4, 4)]),
        (energy.at[pl.ds(4, 4)], o_energy.at[pl.ds(4, 4)]),
    ]
    stores = [pltpu.make_async_copy(s, d, store_sem.at[i]) for i, (s, d) in enumerate(stores)]
    for load in loads:
        load.start()
    loads[0].wait()
    loads[1].wait()
    table = (tz[0], tz[1])
    edges = []
    for xh in range(2):
        done = dot3(split(spec[:, xh].reshape(NZ, 128).T), table)
        edges.append(done[:, BZ:])
        for xl in range(4):
            pot[1 + 4 * xh + xl] = done[32 * xl : 32 * xl + 32, 0:BZ]
    stores[2].start()
    done = dot3(split(spec[:, 2].reshape(NZ, 128).T), (tz[0, :, 0:BZ], tz[1, :, 0:BZ]))
    pot[0] = done[0:32]
    pot[BX + 1] = done[32:64]
    for i in range(2):
        loads[2 + i].wait()
        stores[i].start()
    for load in loads[4:]:
        load.wait()
    row32 = lax.broadcasted_iota(jnp.int32, (BY, BZ), 0)
    lane32 = lax.broadcasted_iota(jnp.int32, (BY, BZ), 1)
    for i in range(BX):
        here = pot[1 + i]
        edge = edges[i // 4][32 * (i % 4) : 32 * (i % 4) + 32]
        pull = [
            pot[i] - pot[i + 2],
            jnp.where(row32 == 0, done[64 + i : 65 + i], pltpu.roll(here, 1, 0))
            - jnp.where(row32 == BY - 1, done[96 + i : 97 + i], pltpu.roll(here, BY - 1, 0)),
            jnp.where(lane32 == 0, edge, pltpu.roll(here, 1, 1))
            - jnp.where(lane32 == BZ - 1, edge, pltpu.roll(here, BZ - 1, 1)),
        ]
        weight = half_step * rho[i]
        work = energy[i]
        for k in range(3):
            push = weight * pull[k]
            mom[k, i] = mom[k, i] + push
            work = work + push * vel[k, i]
        energy[i] = work
        if i == 3:
            stores[3].start()
            stores[4].start()
    stores[5].start()
    stores[6].start()
    for store in stores:
        store.wait()


def local(density, velocity, pressure, species, counts):
    brick = (BX, BY, BZ)
    shape = jax.ShapeDtypeStruct
    anywhere = pl.BlockSpec(memory_space=pl.ANY)
    vmem = pltpu.VMEM
    dma = pltpu.SemaphoreType.DMA
    room = 58 * 1024 * 1024
    table_z, *others = tables()
    gas_shapes = (
        shape(brick, f32),
        shape((3,) + brick, f32),
        shape(brick, f32),
        shape((9,) + brick, f32),
    )
    *gas, waves = pl.pallas_call(
        kernel,
        out_shape=gas_shapes + (shape((16, 3, 16, 128), f32),),
        in_specs=[anywhere] * 11,
        out_specs=(anywhere,) * 5,
        scratch_shapes=[
            vmem((14, BX + 2, BY, BZ), f32),
            vmem((BX + 2, BY, BZ), f32),
            vmem(brick, f32),
            vmem(brick, jnp.int32),
            vmem((2, NZ, 2 * BZ), bf16),
            vmem((2, NY, NY), bf16),
            vmem((2, 48, 128), bf16),
            vmem((2, 128, 48), bf16),
            vmem((48, NY // 2), f32),
            vmem((BX, 16, NY), f32),
            vmem((14,) + brick, f32),
            vmem((16, 2, 16, 128), f32),
            vmem((16, 2, 16, 128), f32),
            vmem((128, NY), f32),
            vmem((128, NY), f32),
            vmem((128, 128), f32),
            vmem((128, 128), f32),
            vmem((128, 128), f32),
            vmem((128, 128), f32),
            vmem((8, 3, 16, 128), f32),
            vmem((2, BX, 16, BZ), f32),
            vmem((2, BX, 16, BZ), f32),
            vmem((BX, 8, 128), f32),
            vmem((BX, 8, 128), f32),
            dma((11,)),
            dma((5,)),
            dma((4, 15)),
            dma((4, 15)),
            dma((15,)),
            dma((15,)),
        ],
        compiler_params=pltpu.CompilerParams(
            collective_id=0, has_side_effects=True, vmem_limit_bytes=room
        ),
        name="step",
    )(density, velocity, pressure, species, counts, table_z, *others)
    return pl.pallas_call(
        finish,
        out_shape=gas_shapes + (shape(brick, f32),),
        in_specs=[anywhere] * 8,
        out_specs=(anywhere,) * 5,
        scratch_shapes=[
            vmem(brick, f32),
            vmem((3,) + brick, f32),
            vmem(brick, f32),
            vmem((3,) + brick, f32),
            vmem(brick, f32),
            vmem((9,) + brick, f32),
            vmem((16, 3, 16, 128), f32),
            vmem((2, NZ, 2 * BZ), bf16),
            vmem((BX + 2, BY, BZ), f32),
            dma((8,)),
            dma((7,)),
        ],
        compiler_params=pltpu.CompilerParams(vmem_limit_bytes=room),
        name="finish",
    )(density, velocity, *gas, waves, table_z)


def solution(mesh):
    in_specs = (
        P("hx", "hy", "ga"),
        P(None, "hx", "hy", "ga"),
        P("hx", "hy", "ga"),
        P(None, "hx", "hy", "ga"),
        P("hx", "hy", "ga"),
    )
    out_specs = (
        P("hx", "hy", "ga"),
        P(None, "hx", "hy", "ga"),
        P("hx", "hy", "ga"),
        P(None, "hx", "hy", "ga"),
        P("hx", "hy", "ga"),
    )
    return jax.shard_map(local, mesh=mesh, in_specs=in_specs, out_specs=out_specs, check_vma=False)
```
